256 devices in a mesh: stat: 8 (over z_lo, core), chan: 32 (over y, z_hi, x).
Axes of the slice: x: 4, y: 4, z: 8 (z_hi: 2, z_lo: 4; z = z_hi * 4 + z_lo), core: 2. Of those that a mesh axis runs over, the one named last changes fastest.
Arguments:
- voltages: bfloat16 [2, 1024, 523, 384], P(None, ('stat', 'chan')), may hold values from -6 to 6
- taps: float32 [12, 384], replicated, may hold values from -1.75 to 1.75
Outputs:
- vis: bfloat16 [384, 2, 1024, 1024], P('chan', None, 'stat')
- gains: float32 [384, 2, 1024], P('chan', None, 'stat')
The draws below stay inside these ranges and needn't reach their ends.
All inputs are finite; a program needn't handle non-finite values.
Results may differ from the reference program's by a relative error of at most 0.0095.
Values may be sent and summed in bfloat16 or wider, within the bound.
A program may use at most 128 MiB of HBM per device.

```python
import math
import jax
import jax.numpy as jnp
from jax import lax

STATIONS = 1024
CHANNELS = 384
FILTER_TAPS = 12
SPECTRA = 512
GAIN_ITERS = 8
SMOOTH_HALF = 3
FRAMES = 523


def levels(stream_key, dims, split, least, top_value):
    gain, own = 1.0, jax.random.fold_in(stream_key, 6)
    for position, blocks in split:
        heights = jnp.exp(jax.random.uniform(jax.random.fold_in(own, position), (blocks,), jnp.float32, least / len(split), top_value / len(split)))
        gain = gain * jnp.repeat(heights, dims[position] // blocks).reshape([-1 if axis == position else 1 for axis in range(len(dims))])
    return gain


def normal_values(stream_key, shape, spread, most, pieces=(), kind=jnp.bfloat16):
    array = spread * jax.random.normal(stream_key, shape, jnp.float32)
    if pieces:
        array = array * levels(stream_key, shape, pieces, -0.22, 0.18)
    return jnp.clip(array, -most, most).astype(kind)


def setup_inputs(seed: int = 0) -> dict:
    arg_keys = jax.random.split(jax.random.key(seed), 3)
    return {
        "voltages": normal_values(arg_keys[0], (2, STATIONS, FRAMES, CHANNELS), 1.0, 6.0, ((1, 256),)),
        "taps": normal_values(arg_keys[1], (FILTER_TAPS, CHANNELS), FILTER_TAPS ** -0.5, 1.75, (), jnp.float32),
    }


EPSILON = 1e-06

def dft_table(length):
    indices = jnp.arange(length, dtype=jnp.int32)
    phases = indices[:, None] * indices[None, :] % length
    angles = phases.astype(jnp.float32) * (2.0 * math.pi / length)
    cosine = jnp.cos(angles) / math.sqrt(length)
    sine = jnp.sin(angles) / math.sqrt(length)
    real_row = jnp.stack([cosine, sine], 1)
    imag_row = jnp.stack([-sine, cosine], 1)
    return jnp.stack([real_row, imag_row], 0).astype(jnp.bfloat16)

def channel_blend(padded, first, count, total):
    indices = first + jnp.arange(count, dtype=jnp.int32)
    summed = jnp.zeros((count,) + padded.shape[1:], jnp.float32)
    weights = jnp.zeros((count,), jnp.float32)
    for offset in range(-SMOOTH_HALF, SMOOTH_HALF + 1):
        factor = 1.0 / (1.0 + abs(offset))
        summed = summed + factor * padded[SMOOTH_HALF + offset:SMOOTH_HALF + offset + count]
        inside = jnp.logical_and(indices + offset >= 0, indices + offset < total)
        weights = weights + factor * inside.astype(jnp.float32)
    return summed / weights.reshape((count,) + (1,) * (padded.ndim - 1))

def gain_combine(products, diagonal, gains_all, gains_own):
    own_real = gains_own[:, 0]
    own_imag = gains_own[:, 1]
    diag_real = diagonal[:, 0]
    diag_imag = diagonal[:, 1]
    real_part = products[:, 0, 0] - products[:, 1, 1] - (diag_real * own_real - diag_imag * own_imag)
    imag_part = products[:, 0, 1] + products[:, 1, 0] - (diag_real * own_imag + diag_imag * own_real)
    power_own = own_real * own_real + own_imag * own_imag
    power_all = lax.optimization_barrier(jnp.sum(gains_all[:, 0] * gains_all[:, 0] + gains_all[:, 1] * gains_all[:, 1], -1, keepdims=True))
    denom = power_all - power_own + EPSILON
    return jnp.stack([real_part / denom, imag_part / denom], 1)

def reference(voltages, taps):
    table = dft_table(CHANNELS)
    blocks = voltages.reshape(2, STATIONS // 64, 64, FRAMES, CHANNELS).transpose(1, 0, 2, 3, 4)

    def channelize(block):
        filtered = jnp.zeros((2, 64, SPECTRA, CHANNELS), jnp.float32)
        for offset in range(FILTER_TAPS):
            filtered = filtered + taps[offset] * block[:, :, offset:offset + SPECTRA, :].astype(jnp.float32)
        filtered = filtered.astype(jnp.bfloat16)
        result = jnp.einsum('akin,istn->akst', table.astype(jnp.float32), filtered.astype(jnp.float32))
        return result.astype(jnp.bfloat16)
    spectra = lax.map(channelize, blocks)
    spectra = spectra.transpose(1, 2, 0, 3, 4).reshape(2, CHANNELS, STATIONS, SPECTRA)

    def correlate(channel):
        right_side = jnp.concatenate([channel[0], channel[1]], -1).astype(jnp.float32)
        left_imag = jnp.concatenate([channel[1], -channel[0]], -1).astype(jnp.float32)
        left_side = jnp.stack([right_side, left_imag], 0)
        product = jnp.einsum('opk,qk->opq', left_side, right_side)
        return (product * (1.0 / SPECTRA)).astype(jnp.bfloat16)
    vis = lax.map(correlate, spectra.transpose(1, 0, 2, 3))
    diagonal = jnp.diagonal(vis, axis1=2, axis2=3).astype(jnp.float32)
    gains = jnp.stack([jnp.ones((CHANNELS, STATIONS), jnp.float32), jnp.zeros((CHANNELS, STATIONS), jnp.float32)], 1)

    def apply_rows(operands):
        return jnp.einsum('ops,is->oip', operands[0].astype(jnp.float32), operands[1], precision=lax.Precision.HIGHEST)
    for sweep in range(GAIN_ITERS):
        products = lax.map(apply_rows, (vis, gains))
        updated = gain_combine(products, diagonal, gains, gains)
        if sweep % 2 == 1:
            updated = 0.5 * (updated + gains)
        padded = jnp.pad(updated, ((SMOOTH_HALF, SMOOTH_HALF), (0, 0), (0, 0)))
        gains = channel_blend(padded, 0, CHANNELS, CHANNELS)
    return (vis, gains)
```

```python
import functools
import math

import jax
import jax.numpy as jnp
import numpy as np
from jax import lax
from jax.experimental import pallas as pl
from jax.experimental.pallas import tpu as pltpu
from jax.sharding import PartitionSpec as P

CHANNELS = 384
STATIONS = 1024
FILTER_TAPS = 12
SPECTRA = 512
GAIN_ITERS = 8
SMOOTH_HALF = 3
EPSILON = 1e-06

MESH = pl.DeviceIdType.MESH
NT = (((1,), (1,)), ((), ()))


def dft_rows(length, groups, depth, share):
    index = np.arange(length)
    angle = (index[:, None] * index[None, :] % length) * (2.0 * math.pi / length)
    cosine = np.cos(angle) / math.sqrt(length)
    sine = np.sin(angle) / math.sqrt(length)
    real_row = np.concatenate([cosine, sine], 1)
    imag_row = np.concatenate([-sine, cosine], 1)
    rows = np.stack([real_row, imag_row], 1)
    rows = rows.reshape(groups, depth, share, 2, 2 * length).transpose(1, 0, 2, 3, 4)
    return jnp.asarray(rows.reshape(2 * length, 2 * length), jnp.bfloat16)


def send_permutation():
    matrix = np.zeros((256, 256), np.float32)
    for p in range(4):
        for th in range(2):
            for k in range(16):
                for a in range(2):
                    matrix[k * 16 + (a * 4 + p) * 2 + th, (p * 2 + th) * 32 + k * 2 + a] = 1.0
    return jnp.asarray(matrix, jnp.bfloat16)


def receive_permutation():
    matrix = np.zeros((256, 256), np.float32)
    for s in range(16):
        for a in range(2):
            for p in range(4):
                for th in range(2):
                    matrix[(a * 2 + th) * 64 + s * 4 + p, s * 16 + (a * 4 + p) * 2 + th] = 1.0
    return jnp.asarray(matrix, jnp.bfloat16)


def channelize_kernel(volt_ref, taps_ref, table_ref, perm_ref, out_ref, wide, filt, stage):
    station = pl.program_id(0)
    frames = SPECTRA + FILTER_TAPS - 1
    for part in range(2):
        wide[pl.ds(0, frames), :] = volt_ref[part, 0].astype(jnp.float32)
        for lane in range(CHANNELS // 128):
            cols = pl.ds(lane * 128, 128)
            weights = [taps_ref[pl.ds(j, 1), cols] for j in range(FILTER_TAPS)]

            def rows(step, _, part=part, lane=lane, cols=cols, weights=weights):
                base = pl.multiple_of(step * 64, 64)
                block = wide[pl.ds(base, 80), cols]
                total = weights[0] * block[0:64]
                for j in range(1, FILTER_TAPS):
                    total = total + weights[j] * block[j : j + 64]
                filt[pl.ds(base, 64), pl.ds(part * CHANNELS + lane * 128, 128)] = total.astype(
                    jnp.bfloat16
                )
                return 0

            lax.fori_loop(0, SPECTRA // 64, rows, 0)
    for block in range(6):
        spectra = lax.dot_general(
            table_ref[pl.ds(block * 128, 128), :],
            filt[...],
            NT,
            preferred_element_type=jnp.float32,
        ).astype(jnp.bfloat16)
        for th in range(2):
            for core in range(2):
                stage[station * 2 + th, pl.ds(block * 128, 128), pl.ds(core * 128, 128)] = spectra[
                    :, (core * 2 + th) * 128 : (core * 2 + th) * 128 + 128
                ]

    @pl.when(station == 3)
    def _():
        for group in range(24):
            rows = jnp.concatenate(
                [stage[i, pl.ds(group * 32, 32), :] for i in range(8)], axis=0
            )
            turned = jnp.dot(
                perm_ref[...], rows, preferred_element_type=jnp.float32
            ).astype(jnp.bfloat16)
            depth, first = group // 6, (group % 6) * 16
            for core in range(2):
                out_ref[depth, core, pl.ds(first, 16)] = turned[
                    :, core * 128 : core * 128 + 128
                ].reshape(16, 16, 128)


def channelize(voltages, taps, table):
    frames = voltages.shape[2]
    return pl.pallas_call(
        channelize_kernel,
        grid=(4,),
        out_shape=jax.ShapeDtypeStruct((4, 2, 96, 16, 128), jnp.bfloat16),
        in_specs=[
            pl.BlockSpec((2, 1, frames, CHANNELS), lambda i: (0, i, 0, 0)),
            pl.BlockSpec((FILTER_TAPS, CHANNELS), lambda i: (0, 0)),
            pl.BlockSpec((2 * CHANNELS, 2 * CHANNELS), lambda i: (0, 0)),
            pl.BlockSpec((256, 256), lambda i: (0, 0)),
        ],
        out_specs=pl.BlockSpec((4, 2, 96, 16, 128), lambda i: (0, 0, 0, 0, 0)),
        scratch_shapes=[
            pltpu.VMEM((528, CHANNELS), jnp.float32),
            pltpu.VMEM((SPECTRA, 2 * CHANNELS), jnp.bfloat16),
            pltpu.VMEM((8, 2 * CHANNELS, 256), jnp.bfloat16),
        ],
        compiler_params=pltpu.CompilerParams(vmem_limit_bytes=48 * 1024 * 1024),
        cost_estimate=pl.CostEstimate(
            flops=2 * 2048 * 768 * 768, bytes_accessed=8 << 20, transcendentals=0
        ),
    )(voltages, taps, table, send_permutation())


def correlate_kernel(core_ref, own_ref, other_ref, perm_ref, out_ref, held):
    depth = pl.program_id(1)

    @pl.when(depth == 0)
    def _():
        for half, source in enumerate((own_ref, other_ref)):

            def group(step, _, half=half, source=source):
                first = pl.multiple_of(step * 16, 16)
                rows = source[pl.ds(first, 16), 0].reshape(256, 128)
                turned = jnp.dot(
                    perm_ref[...], rows, preferred_element_type=jnp.float32
                ).astype(jnp.bfloat16)
                place = pl.ds(pl.multiple_of(step * 64, 64), 64)
                for quarter in range(4):
                    held[place, pl.ds((half * 4 + quarter) * 128, 128)] = turned[
                        quarter * 64 : quarter * 64 + 64
                    ]
                return 0

            lax.fori_loop(0, 16, group, 0)

    first = pl.multiple_of((depth * 2 + core_ref[0]) * 128, 128)
    left = held[pl.ds(first, 128), :]
    pieces = []
    for half in range(2):
        base = half * 512
        pieces += [left[:, base + 256 : base + 512], -left[:, base : base + 256]]
    both = jnp.concatenate([left, jnp.concatenate(pieces, axis=1)], axis=0)
    for block in range(4):
        product = lax.dot_general(
            both, held[pl.ds(block * 256, 256), :], NT, preferred_element_type=jnp.float32
        )
        result = (product * (1.0 / SPECTRA)).astype(jnp.bfloat16)
        for part in range(2):
            out_ref[0, 0, part, :, pl.ds(block * 256, 256)] = result[part * 128 : part * 128 + 128]


def correlate(core, own, other):
    return pl.pallas_call(
        correlate_kernel,
        out_shape=jax.ShapeDtypeStruct((4, 3, 2, 128, STATIONS), jnp.bfloat16),
        grid_spec=pltpu.PrefetchScalarGridSpec(
            num_scalar_prefetch=1,
            grid=(3, 4),
            in_specs=[
                pl.BlockSpec((256, 1, 16, 128), lambda c, z, _: (0, c, 0, 0)),
                pl.BlockSpec((256, 1, 16, 128), lambda c, z, _: (0, c, 0, 0)),
                pl.BlockSpec((256, 256), lambda c, z, _: (0, 0)),
            ],
            out_specs=pl.BlockSpec((1, 1, 2, 128, STATIONS), lambda c, z, _: (z, c, 0, 0, 0)),
            scratch_shapes=[pltpu.VMEM((STATIONS, 2 * SPECTRA), jnp.bfloat16)],
        ),
        compiler_params=pltpu.CompilerParams(vmem_limit_bytes=48 * 1024 * 1024),
        cost_estimate=pl.CostEstimate(
            flops=2 * 3 * 2 * 512 * 1024 * 1024, bytes_accessed=13 << 20, transcendentals=0
        ),
    )(core, own, other, receive_permutation())


def gains_kernel(stat_count, chan_count, vis_ref, out_ref, padded, gains, diag, send_sem, recv_sem):
    share = vis_ref.shape[0]
    rows = vis_ref.shape[2]
    height = 2 * share
    total = chan_count * share
    stations = stat_count * rows
    stat = lax.axis_index("stat")
    chan = lax.axis_index("chan")
    has_low, has_high = chan > 0, chan < chan_count - 1
    peers = [lax.rem(stat + j, stat_count) for j in range(stat_count)]
    sources = [lax.rem(stat + stat_count - j, stat_count) for j in range(stat_count)]
    groups = ((1, None, 0), (0, has_low, -1), (0, has_high, 1))

    for slot in range(2):
        padded[slot, pl.ds(0, 8), :] = jnp.zeros((8, stations), jnp.float32)
        padded[slot, pl.ds(height + 8, 8), :] = jnp.zeros((8, stations), jnp.float32)
    barrier = pltpu.get_barrier_semaphore()
    for first, present, step in groups:

        def greet(first=first, step=step):
            for j in range(first, stat_count):
                pl.semaphore_signal(
                    barrier, inc=1, device_id=(peers[j], chan + step), device_id_type=MESH
                )

        greet() if present is None else pl.when(present)(greet)
    sides = has_low.astype(jnp.int32) + has_high.astype(jnp.int32)
    pl.semaphore_wait(barrier, stat_count - 1 + stat_count * sides)

    own = pl.ds(pl.multiple_of(stat * rows, rows), rows)
    row = lax.broadcasted_iota(jnp.int32, (height, 1), 0)
    even = row % 2 == 0
    sign = jnp.where(even, -1.0, 1.0)
    channel = chan * share + row // 2
    weight = jnp.zeros((height, 1), jnp.float32)
    for m in range(-SMOOTH_HALF, SMOOTH_HALF + 1):
        inside = jnp.logical_and(channel + m >= 0, channel + m < total)
        weight = weight + jnp.where(inside, 1.0 / (1.0 + abs(m)), 0.0)

    def swap(x):
        return jnp.where(even, pltpu.roll(x, height - 1, 0), pltpu.roll(x, 1, 0))

    eye = lax.broadcasted_iota(jnp.int32, (rows, rows), 0) == lax.broadcasted_iota(
        jnp.int32, (rows, rows), 1
    )
    for k in range(share):
        for part in range(2):
            line = jnp.sum(
                jnp.where(eye, vis_ref[k, part, :, own].astype(jnp.float32), 0.0),
                axis=0,
                keepdims=True,
            )
            diag[part, pl.ds(2 * k, 2), :] = jnp.concatenate([line, line], axis=0)
    gains[...] = jnp.broadcast_to(jnp.where(even, 1.0, 0.0), (height, stations))

    def update(odd):
        g = gains[...]
        one = g.astype(jnp.bfloat16).astype(jnp.float32)
        rest = g - one
        two = rest.astype(jnp.bfloat16).astype(jnp.float32)
        three = rest - two
        left = jnp.concatenate(
            [one, two, three, jnp.zeros((8, stations), jnp.float32)], axis=0
        ).astype(jnp.bfloat16)
        real = jnp.zeros((height, rows), jnp.float32)
        imag = jnp.zeros((height, rows), jnp.float32)
        for k in range(share):
            product = lax.dot_general(
                left,
                vis_ref[k].reshape(2 * rows, stations),
                NT,
                preferred_element_type=jnp.float32,
            )
            product = (
                product[0:height]
                + product[height : 2 * height]
                + product[2 * height : 3 * height]
            )
            mine = row // 2 == k
            real = jnp.where(mine, product[:, :rows], real)
            imag = jnp.where(mine, product[:, rows:], imag)
        mine = gains[:, own]
        y = real + sign * swap(imag) - (diag[0] * mine + sign * (diag[1] * swap(mine)))
        power = mine * mine
        power = power + swap(power)
        every = jnp.broadcast_to(jnp.sum(g * g, axis=1, keepdims=True), (height, rows))
        every = every + swap(every)
        u = y / (every - power + EPSILON)
        return jnp.where(odd, 0.5 * (u + mine), u)

    def copies(slot, kind, j, sending):
        where = own if sending else pl.ds(pl.multiple_of(sources[j] * rows, rows), rows)
        middle = (slot, pl.ds(8, height), where)
        source = [middle, (slot, pl.ds(8, 8), where), (slot, pl.ds(height, 8), where)][kind]
        target = [middle, (slot, pl.ds(height + 8, 8), where), (slot, pl.ds(0, 8), where)][kind]
        return pltpu.make_async_remote_copy(
            src_ref=padded.at[source],
            dst_ref=padded.at[target],
            send_sem=send_sem.at[kind, j],
            recv_sem=recv_sem.at[slot, kind, j],
            device_id=(peers[j], chan + (0, -1, 1)[kind]),
            device_id_type=MESH,
        )

    def exchange(slot, kinds):
        for kind, steps, present in kinds:

            def start(kind=kind, steps=steps):
                for j in steps:
                    copies(slot, kind, j, True).start()

            start() if present is None else pl.when(present)(start)
        for kind, steps, present in kinds:
            def wait_out(kind=kind, steps=steps):
                for j in steps:
                    copies(slot, kind, j, True).wait_send()

            def wait_in(kind=kind, steps=steps):
                for j in steps:
                    copies(slot, (0, 2, 1)[kind], j, False).wait_recv()

            if present is None:
                wait_in()
                wait_out()
            else:
                pl.when(present)(wait_in)
                pl.when(present)(wait_out)

    def smooth(slot, columns):
        summed = None
        for m in range(-SMOOTH_HALF, SMOOTH_HALF + 1):
            term = (1.0 / (1.0 + abs(m))) * padded[slot, pl.ds(8 + 2 * m, height), columns]
            summed = term if summed is None else summed + term
        return summed / weight

    everyone = list(range(stat_count))
    full = ((1, everyone, has_low), (2, everyone, has_high), (0, everyone[1:], None))
    edge = ((1, [0], has_low), (2, [0], has_high))

    def iterate(sweep, _):
        slot = lax.rem(sweep, 2)
        padded[slot, pl.ds(8, height), own] = update(slot == 1)
        exchange(slot, full)
        gains[...] = smooth(slot, pl.ds(0, stations))
        return 0

    lax.fori_loop(0, GAIN_ITERS - 1, iterate, 0)
    last = (GAIN_ITERS - 1) % 2
    padded[last, pl.ds(8, height), own] = update(last == 1)
    exchange(last, edge)
    out_ref[...] = smooth(last, own)


def solve_gains(vis):
    share, _, rows, stations = vis.shape
    stat_count, chan_count = lax.axis_size("stat"), lax.axis_size("chan")
    height = 2 * share
    return pl.pallas_call(
        functools.partial(gains_kernel, stat_count, chan_count),
        out_shape=jax.ShapeDtypeStruct((height, rows), jnp.float32),
        in_specs=[pl.BlockSpec(memory_space=pltpu.VMEM)],
        out_specs=pl.BlockSpec(memory_space=pltpu.VMEM),
        scratch_shapes=[
            pltpu.VMEM((2, height + 16, stations), jnp.float32),
            pltpu.VMEM((height, stations), jnp.float32),
            pltpu.VMEM((2, height, rows), jnp.float32),
            pltpu.SemaphoreType.DMA((3, stat_count)),
            pltpu.SemaphoreType.DMA((2, 3, stat_count)),
        ],
        compiler_params=pltpu.CompilerParams(
            collective_id=0, has_side_effects=True, vmem_limit_bytes=40 * 1024 * 1024
        ),
        cost_estimate=pl.CostEstimate(
            flops=8 * 12 * 2 * 80 * 256 * 1024, bytes_accessed=7 << 20, transcendentals=0
        ),
    )(vis)


def local(voltages, taps):
    table = dft_rows(CHANNELS, 32, 4, 3)
    sent = channelize(voltages, taps, table).reshape(256, 3, 16, 128)
    own = lax.all_to_all(sent, ("stat", "chan"), 0, 0, tiled=True)
    other = lax.ppermute(own, "stat", [(i, i ^ 1) for i in range(8)])
    core = (lax.axis_index("stat") % 2).astype(jnp.int32).reshape(1)
    part = correlate(core, own, other)
    lines = [[core + 2 * i for i in range(4)] for core in range(2)]
    vis = lax.all_to_all(part, "stat", 0, 0, axis_index_groups=lines, tiled=True)
    vis = vis.reshape(12, 2, 128, STATIONS)
    gains = solve_gains(vis)
    return vis, gains.reshape(12, 2, 128)


def solution(mesh):
    placed = (P(None, ("stat", "chan"), None, None), P())
    return jax.shard_map(
        local,
        mesh=mesh,
        in_specs=placed,
        out_specs=(P("chan", None, "stat", None), P("chan", None, "stat")),
        check_vma=False,
    )
```

```python
import functools
import math

import jax
import jax.numpy as jnp
import numpy as np
from jax import lax
from jax.experimental import pallas as pl
from jax.experimental.pallas import tpu as pltpu
from jax.sharding import PartitionSpec as P

CHANNELS = 384
STATIONS = 1024
FILTER_TAPS = 12
SPECTRA = 512
GAIN_ITERS = 8
SMOOTH_HALF = 3
EPSILON = 1e-06

MESH = pl.DeviceIdType.MESH
NT = (((1,), (1,)), ((), ()))


def dft_rows(length, groups, depth, share):
    index = np.arange(length)
    angle = (index[:, None] * index[None, :] % length) * (2.0 * math.pi / length)
    cosine = np.cos(angle) / math.sqrt(length)
    sine = np.sin(angle) / math.sqrt(length)
    real_row = np.concatenate([cosine, sine], 1)
    imag_row = np.concatenate([-sine, cosine], 1)
    rows = np.stack([real_row, imag_row], 1)
    rows = rows.reshape(groups, depth, share, 2, 2 * length).transpose(1, 0, 2, 3, 4)
    return jnp.asarray(rows.reshape(2 * length, 2 * length), jnp.bfloat16)


def send_permutation():
    matrix = np.zeros((256, 256), np.float32)
    for p in range(4):
        for th in range(2):
            for k in range(16):
                for a in range(2):
                    matrix[k * 16 + (a * 4 + p) * 2 + th, (p * 2 + th) * 32 + k * 2 + a] = 1.0
    return jnp.asarray(matrix, jnp.bfloat16)


def receive_permutation():
    matrix = np.zeros((256, 256), np.float32)
    for s in range(16):
        for a in range(2):
            for p in range(4):
                for th in range(2):
                    matrix[(a * 2 + th) * 64 + s * 4 + p, s * 16 + (a * 4 + p) * 2 + th] = 1.0
    return jnp.asarray(matrix, jnp.bfloat16)


def channelize_kernel(volt_ref, taps_ref, table_ref, perm_ref, out_ref, wide, filt, stage):
    station = pl.program_id(0)
    frames = SPECTRA + FILTER_TAPS - 1
    for part in range(2):
        wide[pl.ds(0, frames), :] = volt_ref[part, 0].astype(jnp.float32)
        for lane in range(CHANNELS // 128):
            cols = pl.ds(lane * 128, 128)
            weights = [taps_ref[pl.ds(j, 1), cols] for j in range(FILTER_TAPS)]

            def rows(step, _, part=part, lane=lane, cols=cols, weights=weights):
                base = pl.multiple_of(step * 64, 64)
                block = wide[pl.ds(base, 80), cols]
                total = weights[0] * block[0:64]
                for j in range(1, FILTER_TAPS):
                    total = total + weights[j] * block[j : j + 64]
                filt[pl.ds(base, 64), pl.ds(part * CHANNELS + lane * 128, 128)] = total.astype(
                    jnp.bfloat16
                )
                return 0

            lax.fori_loop(0, SPECTRA // 64, rows, 0)
    for block in range(6):
        spectra = lax.dot_general(
            table_ref[pl.ds(block * 128, 128), :],
            filt[...],
            NT,
            preferred_element_type=jnp.float32,
        ).astype(jnp.bfloat16)
        for th in range(2):
            for core in range(2):
                stage[station * 2 + th, pl.ds(block * 128, 128), pl.ds(core * 128, 128)] = spectra[
                    :, (core * 2 + th) * 128 : (core * 2 + th) * 128 + 128
                ]

    @pl.when(station == 3)
    def _():
        for group in range(24):
            rows = jnp.concatenate(
                [stage[i, pl.ds(group * 32, 32), :] for i in range(8)], axis=0
            )
            turned = jnp.dot(
                perm_ref[...], rows, preferred_element_type=jnp.float32
            ).astype(jnp.bfloat16)
            depth, first = group // 6, (group % 6) * 16
            for core in range(2):
                out_ref[depth, core, pl.ds(first, 16)] = turned[
                    :, core * 128 : core * 128 + 128
                ].reshape(16, 16, 128)


def channelize(voltages, taps, table):
    frames = voltages.shape[2]
    return pl.pallas_call(
        channelize_kernel,
        grid=(4,),
        out_shape=jax.ShapeDtypeStruct((4, 2, 96, 16, 128), jnp.bfloat16),
        in_specs=[
            pl.BlockSpec((2, 1, frames, CHANNELS), lambda i: (0, i, 0, 0)),
            pl.BlockSpec((FILTER_TAPS, CHANNELS), lambda i: (0, 0)),
            pl.BlockSpec((2 * CHANNELS, 2 * CHANNELS), lambda i: (0, 0)),
            pl.BlockSpec((256, 256), lambda i: (0, 0)),
        ],
        out_specs=pl.BlockSpec((4, 2, 96, 16, 128), lambda i: (0, 0, 0, 0, 0)),
        scratch_shapes=[
            pltpu.VMEM((528, CHANNELS), jnp.float32),
            pltpu.VMEM((SPECTRA, 2 * CHANNELS), jnp.bfloat16),
            pltpu.VMEM((8, 2 * CHANNELS, 256), jnp.bfloat16),
        ],
        compiler_params=pltpu.CompilerParams(vmem_limit_bytes=48 * 1024 * 1024),
        cost_estimate=pl.CostEstimate(
            flops=2 * 2048 * 768 * 768, bytes_accessed=8 << 20, transcendentals=0
        ),
    )(voltages, taps, table, send_permutation())


def exchange_kernel(
    stat_count,
    chan_count,
    own_ref,
    perm_ref,
    out_ref,
    gains_ref,
    other,
    held,
    stage,
    vis,
    turned,
    padded,
    gains,
    diag,
    pair_send,
    pair_recv,
    vis_send,
    vis_recv,
    out_sem,
    send_sem,
    recv_sem,
):
    sources, depth = own_ref.shape[0], own_ref.shape[1]
    share, _, rows, stations = vis.shape
    height = 2 * share
    total = chan_count * share
    stat = lax.axis_index("stat")
    chan = lax.axis_index("chan")
    line, core = stat // 2, stat % 2
    has_low, has_high = chan > 0, chan < chan_count - 1
    peers = [lax.rem(stat + j, stat_count) for j in range(stat_count)]
    senders = [lax.rem(stat + stat_count - j, stat_count) for j in range(stat_count)]

    def partner(d):
        return 2 * ((line // 2 + (1, 1, 0, 0)[d]) % 2) + (line % 2 + (0, 1, 1, 0)[d]) % 2

    for slot in range(2):
        padded[slot, pl.ds(0, 8), :] = jnp.zeros((8, stations), jnp.float32)
        padded[slot, pl.ds(height + 8, 8), :] = jnp.zeros((8, stations), jnp.float32)
    barrier = pltpu.get_barrier_semaphore()
    for first, present, step in ((1, None, 0), (0, has_low, -1), (0, has_high, 1)):

        def greet(first=first, step=step):
            for j in range(first, stat_count):
                pl.semaphore_signal(
                    barrier, inc=1, device_id=(peers[j], chan + step), device_id_type=MESH
                )

        greet() if present is None else pl.when(present)(greet)
    sides = has_low.astype(jnp.int32) + has_high.astype(jnp.int32)
    pl.semaphore_wait(barrier, stat_count - 1 + stat_count * sides)

    def pair_copy(c):
        return pltpu.make_async_remote_copy(
            src_ref=own_ref.at[:, c],
            dst_ref=other.at[c],
            send_sem=pair_send.at[c],
            recv_sem=pair_recv.at[c],
            device_id=(line * 2 + 1 - core, chan),
            device_id_type=MESH,
        )

    for c in range(depth):
        pair_copy(c).start()

    def assemble(half, source):
        def group(step, _):
            first = pl.multiple_of(step * 16, 16)
            block = source[pl.ds(first, 16)].reshape(256, 128)
            moved = jnp.dot(perm_ref[...], block, preferred_element_type=jnp.float32).astype(
                jnp.bfloat16
            )
            place = pl.ds(pl.multiple_of(step * 64, 64), 64)
            for quarter in range(4):
                held[place, pl.ds((half * 4 + quarter) * 128, 128)] = moved[
                    quarter * 64 : quarter * 64 + 64
                ]
            return 0

        lax.fori_loop(0, sources // 16, group, 0)

    def vis_copy(c, d, sending):
        return pltpu.make_async_remote_copy(
            src_ref=stage.at[c * 3 + d],
            dst_ref=vis.at[(line if sending else partner(d)) * depth + c],
            send_sem=vis_send.at[c, d],
            recv_sem=vis_recv.at[c, d],
            device_id=(partner(d) * 2 + core, chan),
            device_id_type=MESH,
        )

    width = min(256, stations)

    def correlate(c, _):
        assemble(0, own_ref.at[:, c])
        pair_copy(c).wait_recv()
        assemble(1, other.at[c])
        for d in range(4):
            first = pl.multiple_of((partner(d) * 2 + core) * rows, rows)
            left = held[pl.ds(first, rows), :]
            pieces = []
            for half in range(2):
                base = half * 512
                pieces += [left[:, base + 256 : base + 512], -left[:, base : base + 256]]
            both = jnp.concatenate([left, jnp.concatenate(pieces, axis=1)], axis=0)
            for block in range(stations // width):
                product = lax.dot_general(
                    both,
                    held[pl.ds(block * width, width), :],
                    NT,
                    preferred_element_type=jnp.float32,
                )
                result = (product * (1.0 / SPECTRA)).astype(jnp.bfloat16)
                columns = pl.ds(block * width, width)
                for part in range(2):
                    piece = result[part * rows : part * rows + rows]
                    if d < 3:
                        stage[c * 3 + d, part, :, columns] = piece
                    else:
                        vis[line * depth + c, part, :, columns] = piece
            if d < 3:
                vis_copy(c, d, True).start()
        return 0

    lax.fori_loop(0, depth, correlate, 0)

    own = pl.ds(pl.multiple_of(stat * rows, rows), rows)
    row = lax.broadcasted_iota(jnp.int32, (height, 1), 0)
    even = row % 2 == 0
    sign = jnp.where(even, -1.0, 1.0)
    channel = chan * share + row // 2
    weight = jnp.zeros((height, 1), jnp.float32)
    for m in range(-SMOOTH_HALF, SMOOTH_HALF + 1):
        inside = jnp.logical_and(channel + m >= 0, channel + m < total)
        weight = weight + jnp.where(inside, 1.0 / (1.0 + abs(m)), 0.0)

    def swap(x):
        return jnp.where(even, pltpu.roll(x, height - 1, 0), pltpu.roll(x, 1, 0))

    eye = lax.broadcasted_iota(jnp.int32, (rows, rows), 0) == lax.broadcasted_iota(
        jnp.int32, (rows, rows), 1
    )

    def split(g):
        one = g.astype(jnp.bfloat16).astype(jnp.float32)
        rest = g - one
        two = rest.astype(jnp.bfloat16).astype(jnp.float32)
        three = rest - two
        return jnp.concatenate(
            [one, two, three, jnp.zeros((8, stations), jnp.float32)], axis=0
        ).astype(jnp.bfloat16)

    def multiply(left, k, real, imag):
        product = jnp.dot(left, turned[k], preferred_element_type=jnp.float32)
        product = (
            product[0:height] + product[height : 2 * height] + product[2 * height : 3 * height]
        )
        mine = row // 2 == k
        return jnp.where(mine, product[:, :rows], real), jnp.where(mine, product[:, rows:], imag)

    def out_copy(k):
        return pltpu.make_async_copy(vis.at[k], out_ref.at[k], out_sem.at[k])

    gains[...] = jnp.broadcast_to(jnp.where(even, 1.0, 0.0), (height, stations))
    left = split(gains[...])
    zero = jnp.zeros((height, rows), jnp.float32)

    def arrive(c, carry):
        real, imag, diag_real, diag_imag = carry
        for d in (3, 0, 1, 2):
            if d < 3:
                vis_copy(c, d, False).wait_recv()
            k = partner(d) * depth + c
            out_copy(k).start()
            turned[k] = vis[k].reshape(2 * rows, stations).T
            mine = row // 2 == k
            lines = [
                jnp.sum(
                    jnp.where(eye, vis[k, part, :, own].astype(jnp.float32), 0.0),
                    axis=0,
                    keepdims=True,
                )
                for part in range(2)
            ]
            diag_real = jnp.where(mine, lines[0], diag_real)
            diag_imag = jnp.where(mine, lines[1], diag_imag)
            real, imag = multiply(left, k, real, imag)
        return real, imag, diag_real, diag_imag

    real, imag, diag_real, diag_imag = lax.fori_loop(0, depth, arrive, (zero, zero, zero, zero))
    diag[0] = diag_real
    diag[1] = sign * diag_imag

    def finish(odd, real, imag):
        g = gains[...]
        mine = gains[:, own]
        y = real + sign * swap(imag) - (diag[0] * mine + diag[1] * swap(mine))
        power = mine * mine
        power = power + swap(power)
        every = jnp.broadcast_to(jnp.sum(g * g, axis=1, keepdims=True), (height, rows))
        every = every + swap(every)
        u = y / (every - power + EPSILON)
        return jnp.where(odd, 0.5 * (u + mine), u)

    def copies(slot, kind, j, sending):
        where = own if sending else pl.ds(pl.multiple_of(senders[j] * rows, rows), rows)
        middle = (slot, pl.ds(8, height), where)
        source = [middle, (slot, pl.ds(8, 8), where), (slot, pl.ds(height, 8), where)][kind]
        target = [middle, (slot, pl.ds(height + 8, 8), where), (slot, pl.ds(0, 8), where)][kind]
        return pltpu.make_async_remote_copy(
            src_ref=padded.at[source],
            dst_ref=padded.at[target],
            send_sem=send_sem.at[kind, j],
            recv_sem=recv_sem.at[slot, kind, j],
            device_id=(peers[j], chan + (0, -1, 1)[kind]),
            device_id_type=MESH,
        )

    def exchange(slot, kinds):
        for kind, steps, present in kinds:

            def start(kind=kind, steps=steps):
                for j in steps:
                    copies(slot, kind, j, True).start()

            start() if present is None else pl.when(present)(start)
        for kind, steps, present in kinds:
            def wait_out(kind=kind, steps=steps):
                for j in steps:
                    copies(slot, kind, j, True).wait_send()

            def wait_in(kind=kind, steps=steps):
                for j in steps:
                    copies(slot, (0, 2, 1)[kind], j, False).wait_recv()

            if present is None:
                wait_in()
                wait_out()
            else:
                pl.when(present)(wait_in)
                pl.when(present)(wait_out)

    def smooth(slot, columns):
        summed = None
        for m in range(-SMOOTH_HALF, SMOOTH_HALF + 1):
            term = (1.0 / (1.0 + abs(m))) * padded[slot, pl.ds(8 + 2 * m, height), columns]
            summed = term if summed is None else summed + term
        return summed / weight

    everyone = list(range(stat_count))
    full = ((1, everyone, has_low), (2, everyone, has_high), (0, everyone[1:], None))
    edge = ((1, [0], has_low), (2, [0], has_high))

    def iterate(sweep, carry):
        slot = lax.rem(sweep, 2)
        padded[slot, pl.ds(8, height), own] = finish(slot == 1, *carry)
        exchange(slot, full)
        g = smooth(slot, pl.ds(0, stations))
        gains[...] = g
        left = split(g)
        real, imag = zero, zero
        for k in range(share):
            real, imag = multiply(left, k, real, imag)
        return real, imag

    real, imag = lax.fori_loop(0, GAIN_ITERS - 1, iterate, (real, imag))
    last = (GAIN_ITERS - 1) % 2
    padded[last, pl.ds(8, height), own] = finish(last == 1, real, imag)
    exchange(last, edge)
    gains_ref[...] = smooth(last, own)
    for c in range(depth):
        pair_copy(c).wait_send()
        for d in range(3):
            vis_copy(c, d, True).wait_send()
    for k in range(share):
        out_copy(k).wait()


def correlate_and_solve(own):
    sources, depth = own.shape[:2]
    stations = 4 * sources
    stat_count, chan_count = lax.axis_size("stat"), lax.axis_size("chan")
    share, rows = 4 * depth, stations // stat_count
    height = 2 * share
    return pl.pallas_call(
        functools.partial(exchange_kernel, stat_count, chan_count),
        out_shape=(
            jax.ShapeDtypeStruct((share, 2, rows, stations), jnp.bfloat16),
            jax.ShapeDtypeStruct((height, rows), jnp.float32),
        ),
        in_specs=[pl.BlockSpec(memory_space=pltpu.VMEM)] * 2,
        out_specs=(
            pl.BlockSpec(memory_space=pl.ANY),
            pl.BlockSpec(memory_space=pltpu.VMEM),
        ),
        scratch_shapes=[
            pltpu.VMEM((depth, sources, 16, 128), jnp.bfloat16),
            pltpu.VMEM((stations, 2 * SPECTRA), jnp.bfloat16),
            pltpu.VMEM((3 * depth, 2, rows, stations), jnp.bfloat16),
            pltpu.VMEM((share, 2, rows, stations), jnp.bfloat16),
            pltpu.VMEM((share, stations, 2 * rows), jnp.bfloat16),
            pltpu.VMEM((2, height + 16, stations), jnp.float32),
            pltpu.VMEM((height, stations), jnp.float32),
            pltpu.VMEM((2, height, rows), jnp.float32),
            pltpu.SemaphoreType.DMA((depth,)),
            pltpu.SemaphoreType.DMA((depth,)),
            pltpu.SemaphoreType.DMA((depth, 3)),
            pltpu.SemaphoreType.DMA((depth, 3)),
            pltpu.SemaphoreType.DMA((share,)),
            pltpu.SemaphoreType.DMA((3, stat_count)),
            pltpu.SemaphoreType.DMA((2, 3, stat_count)),
        ],
        compiler_params=pltpu.CompilerParams(
            collective_id=0, has_side_effects=True, vmem_limit_bytes=48 * 1024 * 1024
        ),
        cost_estimate=pl.CostEstimate(
            flops=2 * 3 * 2 * 512 * 1024 * 1024, bytes_accessed=12 << 20, transcendentals=0
        ),
    )(own, receive_permutation())


def local(voltages, taps):
    table = dft_rows(CHANNELS, 32, 4, 3)
    sent = channelize(voltages, taps, table).reshape(256, 3, 16, 128)
    own = lax.all_to_all(sent, ("stat", "chan"), 0, 0, tiled=True)
    vis, gains = correlate_and_solve(own)
    return vis, gains.reshape(12, 2, 128)


def solution(mesh):
    placed = (P(None, ("stat", "chan"), None, None), P())
    return jax.shard_map(
        local,
        mesh=mesh,
        in_specs=placed,
        out_specs=(P("chan", None, "stat", None), P("chan", None, "stat")),
        check_vma=False,
    )
```

```python
import functools
import math

import jax
import jax.numpy as jnp
import numpy as np
from jax import lax
from jax.experimental import pallas as pl
from jax.experimental.pallas import tpu as pltpu
from jax.sharding import PartitionSpec as P

CHANNELS = 384
STATIONS = 1024
FILTER_TAPS = 12
SPECTRA = 512
GAIN_ITERS = 8
SMOOTH_HALF = 3
EPSILON = 1e-06

MESH = pl.DeviceIdType.MESH
NT = (((1,), (1,)), ((), ()))


def dft_rows(length, groups, depth, share):
    index = np.arange(length)
    angle = (index[:, None] * index[None, :] % length) * (2.0 * math.pi / length)
    cosine = np.cos(angle) / math.sqrt(length)
    sine = np.sin(angle) / math.sqrt(length)
    real_row = np.concatenate([cosine, sine], 1)
    imag_row = np.concatenate([-sine, cosine], 1)
    rows = np.stack([real_row, imag_row], 1)
    rows = rows.reshape(groups, depth, share, 2, 2 * length).transpose(1, 0, 2, 3, 4)
    return jnp.asarray(rows.reshape(2 * length, 2 * length), jnp.bfloat16)


def send_permutation():
    matrix = np.zeros((256, 256), np.float32)
    for p in range(4):
        for th in range(2):
            for k in range(16):
                for a in range(2):
                    matrix[k * 16 + (a * 4 + p) * 2 + th, (p * 2 + th) * 32 + k * 2 + a] = 1.0
    return jnp.asarray(matrix, jnp.bfloat16)


def receive_permutation():
    matrix = np.zeros((256, 256), np.float32)
    for s in range(16):
        for a in range(2):
            for p in range(4):
                for th in range(2):
                    matrix[(a * 2 + th) * 64 + s * 4 + p, s * 16 + (a * 4 + p) * 2 + th] = 1.0
    return jnp.asarray(matrix, jnp.bfloat16)


def channelize_kernel(volt_ref, taps_ref, table_ref, perm_ref, out_ref, wide, filt, stage):
    station = pl.program_id(0)
    frames = SPECTRA + FILTER_TAPS - 1
    for part in range(2):
        for lane in range(CHANNELS // 128):
            wide[lane, pl.ds(0, frames), :] = volt_ref[part, 0, :, pl.ds(lane * 128, 128)].astype(
                jnp.float32
            )
        for lane in range(CHANNELS // 128):
            weights = [taps_ref[pl.ds(j, 1), pl.ds(lane * 128, 128)] for j in range(FILTER_TAPS)]

            def rows(step, _, part=part, lane=lane, weights=weights):
                base = step * 128
                total = weights[0] * wide[lane, pl.ds(base, 128), :]
                for j in range(1, FILTER_TAPS):
                    total = total + weights[j] * wide[lane, pl.ds(base + j, 128), :]
                filt[pl.ds(base, 128), pl.ds(part * CHANNELS + lane * 128, 128)] = total.astype(
                    jnp.bfloat16
                )
                return 0

            for step in range(SPECTRA // 128):
                rows(step, 0)
    for block in range(1):
        spectra = lax.dot_general(
            table_ref[pl.ds(block * 768, 768), :],
            filt[...],
            NT,
            preferred_element_type=jnp.float32,
        ).astype(jnp.bfloat16)
        for th in range(2):
            for core in range(2):
                stage[station * 2 + th, pl.ds(block * 768, 768), pl.ds(core * 128, 128)] = spectra[
                    :, (core * 2 + th) * 128 : (core * 2 + th) * 128 + 128
                ]

    @pl.when(station == 3)
    def _():
        for group in range(24):
            rows = jnp.concatenate(
                [stage[i, pl.ds(group * 32, 32), :] for i in range(8)], axis=0
            )
            turned = jnp.dot(
                perm_ref[...], rows, preferred_element_type=jnp.float32
            ).astype(jnp.bfloat16)
            depth, first = group // 6, (group % 6) * 16
            for core in range(2):
                out_ref[depth, core, pl.ds(first, 16)] = turned[
                    :, core * 128 : core * 128 + 128
                ].reshape(16, 16, 128)


def channelize(voltages, taps, table):
    frames = voltages.shape[2]
    return pl.pallas_call(
        channelize_kernel,
        grid=(4,),
        out_shape=jax.ShapeDtypeStruct((4, 2, 96, 16, 128), jnp.bfloat16),
        in_specs=[
            pl.BlockSpec((2, 1, frames, CHANNELS), lambda i: (0, i, 0, 0)),
            pl.BlockSpec((FILTER_TAPS, CHANNELS), lambda i: (0, 0)),
            pl.BlockSpec((2 * CHANNELS, 2 * CHANNELS), lambda i: (0, 0)),
            pl.BlockSpec((256, 256), lambda i: (0, 0)),
        ],
        out_specs=pl.BlockSpec((4, 2, 96, 16, 128), lambda i: (0, 0, 0, 0, 0)),
        scratch_shapes=[
            pltpu.VMEM((CHANNELS // 128, 528, 128), jnp.float32),
            pltpu.VMEM((SPECTRA, 2 * CHANNELS), jnp.bfloat16),
            pltpu.VMEM((8, 2 * CHANNELS, 256), jnp.bfloat16),
        ],
        compiler_params=pltpu.CompilerParams(vmem_limit_bytes=48 * 1024 * 1024),
        cost_estimate=pl.CostEstimate(
            flops=2 * 2048 * 768 * 768, bytes_accessed=8 << 20, transcendentals=0
        ),
    )(voltages, taps, table, send_permutation())


def exchange_kernel(
    stat_count,
    chan_count,
    own_ref,
    perm_ref,
    out_ref,
    gains_ref,
    other,
    held,
    stage,
    flip,
    vis,
    turned,
    padded,
    gains,
    diag,
    pair_send,
    pair_recv,
    vis_send,
    vis_recv,
    flip_send,
    flip_recv,
    out_sem,
    send_sem,
    recv_sem,
):
    sources, depth = own_ref.shape[0], own_ref.shape[1]
    share, _, rows, stations = vis.shape
    height = 2 * share
    total = chan_count * share
    stat = lax.axis_index("stat")
    chan = lax.axis_index("chan")
    line, core = stat // 2, stat % 2
    has_low, has_high = chan > 0, chan < chan_count - 1
    peers = [lax.rem(stat + j, stat_count) for j in range(stat_count)]
    senders = [lax.rem(stat + stat_count - j, stat_count) for j in range(stat_count)]

    def partner(d):
        return 2 * ((line // 2 + (1, 1, 0, 0)[d]) % 2) + (line % 2 + (0, 1, 1, 0)[d]) % 2

    for slot in range(2):
        padded[slot, pl.ds(0, 8), :] = jnp.zeros((8, stations), jnp.float32)
        padded[slot, pl.ds(height + 8, 8), :] = jnp.zeros((8, stations), jnp.float32)
    barrier = pltpu.get_barrier_semaphore()
    for first, present, step in ((1, None, 0), (0, has_low, -1), (0, has_high, 1)):

        def greet(first=first, step=step):
            for j in range(first, stat_count):
                pl.semaphore_signal(
                    barrier, inc=1, device_id=(peers[j], chan + step), device_id_type=MESH
                )

        greet() if present is None else pl.when(present)(greet)
    sides = has_low.astype(jnp.int32) + has_high.astype(jnp.int32)
    pl.semaphore_wait(barrier, stat_count - 1 + stat_count * sides)

    def pair_copy(c):
        return pltpu.make_async_remote_copy(
            src_ref=own_ref.at[:, c],
            dst_ref=other.at[c],
            send_sem=pair_send.at[c],
            recv_sem=pair_recv.at[c],
            device_id=(line * 2 + 1 - core, chan),
            device_id_type=MESH,
        )

    for c in range(depth):
        pair_copy(c).start()

    def assemble(half, source):
        def group(step, _):
            first = pl.multiple_of(step * 16, 16)
            block = source[pl.ds(first, 16)].reshape(256, 128)
            moved = jnp.dot(perm_ref[...], block, preferred_element_type=jnp.float32).astype(
                jnp.bfloat16
            )
            place = pl.ds(pl.multiple_of(step * 64, 64), 64)
            for quarter in range(4):
                held[place, pl.ds((half * 4 + quarter) * 128, 128)] = moved[
                    quarter * 64 : quarter * 64 + 64
                ]
            return 0

        lax.fori_loop(0, sources // 16, group, 0)

    inner = (line + 1) // 2 % 2 == 1
    outer = jnp.logical_not(inner)
    first_core, second_core = core == 0, core == 1

    def columns_of(place, width):
        return pl.ds(pl.multiple_of(place * rows, rows), width * rows)

    def vis_copy(c, d, kind, sending):
        target = partner(d) if sending else line
        columns = (
            columns_of(4 * (1 - target // 2), 4),
            columns_of(2 * target, 2),
            columns_of(2 * target + 1, 1),
            columns_of(2 * (target + 1 - 2 * (target % 2)), 2),
            pl.ds(0, stations),
        )[kind]
        place = (line if sending else partner(d)) * depth + c
        return pltpu.make_async_remote_copy(
            src_ref=stage.at[c * 3 + d, :, :, columns],
            dst_ref=vis.at[place, :, :, columns],
            send_sem=vis_send.at[c, d, (0, 1, 1, 2, 0)[kind]],
            recv_sem=vis_recv.at[c, d, (0, 1, 1, 2, 0)[kind]],
            device_id=(partner(d) * 2 + core, chan),
            device_id_type=MESH,
        )

    def vis_pieces(d, sending):
        if d == 2:
            return ((4, None),)
        meets_inner = inner if (d == 1) or not sending else outer
        return ((3, meets_inner), (1, first_core), (2, second_core), (0, None))

    def guarded(present, action):
        action() if present is None else pl.when(present)(action)

    def flip_copy(c, d, kind, sending):
        near = partner(2)
        k = partner(d) * depth + c
        if sending:
            columns = columns_of(stat, 1)
            device = (near * 2, near * 2 + 1, line * 2 + 1)[kind]
            slot = 2 if kind == 2 else core
            step = d if kind == 2 else 1 - d
        else:
            columns = columns_of((near * 2, near * 2 + 1, line * 2)[kind], 1)
            device, slot, step = stat, kind, d
        return pltpu.make_async_remote_copy(
            src_ref=flip.at[c, d, kind],
            dst_ref=vis.at[k, :, :, columns],
            send_sem=flip_send.at[c, d, kind],
            recv_sem=flip_recv.at[c, step, slot],
            device_id=(device, chan),
            device_id_type=MESH,
        )

    def send_flipped(c, d, kind):
        near = partner(2)
        columns = columns_of((near * 2, near * 2 + 1, line * 2 + 1)[kind], 1)
        k = partner(d) * depth + c
        flip[c, d, kind, 0] = vis[k, 0, :, columns].T
        flip[c, d, kind, 1] = -vis[k, 1, :, columns].T
        flip_copy(c, d, kind, True).start()

    def receive(c, d):
        if d == 2:
            vis_copy(c, d, 4, False).wait_recv()
            return

        def neighbour():
            vis_copy(c, d, 3, False).wait_recv()
            send_flipped(c, d, 0)
            send_flipped(c, d, 1)

        def pair():
            vis_copy(c, d, 1, False).wait_recv()
            send_flipped(c, d, 2)

        def from_neighbour():
            flip_copy(c, d, 0, False).wait_recv()
            flip_copy(c, d, 1, False).wait_recv()

        def from_pair():
            vis_copy(c, d, 2, False).wait_recv()
            flip_copy(c, d, 2, False).wait_recv()

        pl.when(inner)(neighbour)
        pl.when(first_core)(pair)
        vis_copy(c, d, 0, False).wait_recv()
        pl.when(outer)(from_neighbour)
        pl.when(second_core)(from_pair)

    width = min(256, stations)

    def correlate(c, _):
        assemble(0, own_ref.at[:, c])
        pair_copy(c).wait_recv()
        assemble(1, other.at[c])
        for d in range(4):
            first = pl.multiple_of((partner(d) * 2 + core) * rows, rows)
            left = held[pl.ds(first, rows), :]
            pieces = []
            for half in range(2):
                base = half * 512
                pieces += [left[:, base + 256 : base + 512], -left[:, base : base + 256]]
            both = jnp.concatenate([left, jnp.concatenate(pieces, axis=1)], axis=0)
            for block in range(stations // width):
                product = lax.dot_general(
                    both,
                    held[pl.ds(block * width, width), :],
                    NT,
                    preferred_element_type=jnp.float32,
                )
                result = (product * (1.0 / SPECTRA)).astype(jnp.bfloat16)
                columns = pl.ds(block * width, width)
                for part in range(2):
                    piece = result[part * rows : part * rows + rows]
                    if d < 3:
                        stage[c * 3 + d, part, :, columns] = piece
                    else:
                        vis[line * depth + c, part, :, columns] = piece
            if d < 3:
                for kind, present in vis_pieces(d, True):
                    guarded(present, lambda: vis_copy(c, d, kind, True).start())
        return 0

    lax.fori_loop(0, depth, correlate, 0)

    own = pl.ds(pl.multiple_of(stat * rows, rows), rows)
    row = lax.broadcasted_iota(jnp.int32, (height, 1), 0)
    even = row % 2 == 0
    sign = jnp.where(even, -1.0, 1.0)
    channel = chan * share + row // 2
    weight = jnp.zeros((height, 1), jnp.float32)
    for m in range(-SMOOTH_HALF, SMOOTH_HALF + 1):
        inside = jnp.logical_and(channel + m >= 0, channel + m < total)
        weight = weight + jnp.where(inside, 1.0 / (1.0 + abs(m)), 0.0)

    def swap(x):
        return jnp.where(even, pltpu.roll(x, height - 1, 0), pltpu.roll(x, 1, 0))

    eye = lax.broadcasted_iota(jnp.int32, (rows, rows), 0) == lax.broadcasted_iota(
        jnp.int32, (rows, rows), 1
    )

    def split(g):
        one = g.astype(jnp.bfloat16).astype(jnp.float32)
        rest = g - one
        two = rest.astype(jnp.bfloat16).astype(jnp.float32)
        three = rest - two
        return jnp.concatenate(
            [one, two, three, jnp.zeros((8, stations), jnp.float32)], axis=0
        ).astype(jnp.bfloat16)

    def multiply(left, k, real, imag):
        product = jnp.dot(left, turned[k], preferred_element_type=jnp.float32)
        product = (
            product[0:height] + product[height : 2 * height] + product[2 * height : 3 * height]
        )
        mine = row // 2 == k
        return jnp.where(mine, product[:, :rows], real), jnp.where(mine, product[:, rows:], imag)

    def out_copy(k):
        return pltpu.make_async_copy(vis.at[k], out_ref.at[k], out_sem.at[k])

    gains[...] = jnp.broadcast_to(jnp.where(even, 1.0, 0.0), (height, stations))
    left = split(gains[...])
    zero = jnp.zeros((height, rows), jnp.float32)

    def arrive(c, carry):
        real, imag, diag_real, diag_imag = carry
        for d in (3, 2, 0, 1):
            if d < 3:
                receive(c, d)
            k = partner(d) * depth + c
            out_copy(k).start()
            turned[k] = vis[k].reshape(2 * rows, stations).T
            mine = row // 2 == k
            lines = [
                jnp.sum(
                    jnp.where(eye, vis[k, part, :, own].astype(jnp.float32), 0.0),
                    axis=0,
                    keepdims=True,
                )
                for part in range(2)
            ]
            diag_real = jnp.where(mine, lines[0], diag_real)
            diag_imag = jnp.where(mine, lines[1], diag_imag)
            real, imag = multiply(left, k, real, imag)
        return real, imag, diag_real, diag_imag

    real, imag, diag_real, diag_imag = lax.fori_loop(0, depth, arrive, (zero, zero, zero, zero))
    diag[0] = diag_real
    diag[1] = sign * diag_imag

    def finish(odd, real, imag):
        g = gains[...]
        mine = gains[:, own]
        y = real + sign * swap(imag) - (diag[0] * mine + diag[1] * swap(mine))
        power = mine * mine
        power = power + swap(power)
        every = jnp.broadcast_to(jnp.sum(g * g, axis=1, keepdims=True), (height, rows))
        every = every + swap(every)
        u = y / (every - power + EPSILON)
        return jnp.where(odd, 0.5 * (u + mine), u)

    def copies(slot, kind, j, sending):
        where = own if sending else pl.ds(pl.multiple_of(senders[j] * rows, rows), rows)
        middle = (slot, pl.ds(8, height), where)
        source = [middle, (slot, pl.ds(8, 8), where), (slot, pl.ds(height, 8), where)][kind]
        target = [middle, (slot, pl.ds(height + 8, 8), where), (slot, pl.ds(0, 8), where)][kind]
        return pltpu.make_async_remote_copy(
            src_ref=padded.at[source],
            dst_ref=padded.at[target],
            send_sem=send_sem.at[kind, j],
            recv_sem=recv_sem.at[slot, kind, j],
            device_id=(peers[j], chan + (0, -1, 1)[kind]),
            device_id_type=MESH,
        )

    def exchange(slot, kinds):
        for kind, steps, present in kinds:

            def start(kind=kind, steps=steps):
                for j in steps:
                    copies(slot, kind, j, True).start()

            start() if present is None else pl.when(present)(start)
        for kind, steps, present in kinds:
            def wait_out(kind=kind, steps=steps):
                for j in steps:
                    copies(slot, kind, j, True).wait_send()

            def wait_in(kind=kind, steps=steps):
                for j in steps:
                    copies(slot, (0, 2, 1)[kind], j, False).wait_recv()

            if present is None:
                wait_in()
                wait_out()
            else:
                pl.when(present)(wait_in)
                pl.when(present)(wait_out)

    def smooth(slot, columns):
        summed = None
        for m in range(-SMOOTH_HALF, SMOOTH_HALF + 1):
            term = (1.0 / (1.0 + abs(m))) * padded[slot, pl.ds(8 + 2 * m, height), columns]
            summed = term if summed is None else summed + term
        return summed / weight

    everyone = list(range(stat_count))
    full = ((1, everyone, has_low), (2, everyone, has_high), (0, everyone[1:], None))
    edge = ((1, [0], has_low), (2, [0], has_high))

    def iterate(sweep, carry):
        slot = lax.rem(sweep, 2)
        padded[slot, pl.ds(8, height), own] = finish(slot == 1, *carry)
        exchange(slot, full)
        g = smooth(slot, pl.ds(0, stations))
        gains[...] = g
        left = split(g)
        real, imag = zero, zero
        for k in range(share):
            real, imag = multiply(left, k, real, imag)
        return real, imag

    real, imag = lax.fori_loop(0, GAIN_ITERS - 1, iterate, (real, imag))
    last = (GAIN_ITERS - 1) % 2
    padded[last, pl.ds(8, height), own] = finish(last == 1, real, imag)
    exchange(last, edge)
    gains_ref[...] = smooth(last, own)
    for c in range(depth):
        pair_copy(c).wait_send()
        for d in range(3):
            for kind, present in vis_pieces(d, True):
                guarded(present, lambda: vis_copy(c, d, kind, True).wait_send())
        for d in range(2):
            for kind, present in ((0, inner), (1, inner), (2, first_core)):
                guarded(present, lambda: flip_copy(c, d, kind, True).wait_send())
    for k in range(share):
        out_copy(k).wait()


def correlate_and_solve(own):
    sources, depth = own.shape[:2]
    stations = 4 * sources
    stat_count, chan_count = lax.axis_size("stat"), lax.axis_size("chan")
    share, rows = 4 * depth, stations // stat_count
    height = 2 * share
    return pl.pallas_call(
        functools.partial(exchange_kernel, stat_count, chan_count),
        out_shape=(
            jax.ShapeDtypeStruct((share, 2, rows, stations), jnp.bfloat16),
            jax.ShapeDtypeStruct((height, rows), jnp.float32),
        ),
        in_specs=[pl.BlockSpec(memory_space=pltpu.VMEM)] * 2,
        out_specs=(
            pl.BlockSpec(memory_space=pl.ANY),
            pl.BlockSpec(memory_space=pltpu.VMEM),
        ),
        scratch_shapes=[
            pltpu.VMEM((depth, sources, 16, 128), jnp.bfloat16),
            pltpu.VMEM((stations, 2 * SPECTRA), jnp.bfloat16),
            pltpu.VMEM((3 * depth, 2, rows, stations), jnp.bfloat16),
            pltpu.VMEM((depth, 2, 3, 2, rows, rows), jnp.bfloat16),
            pltpu.VMEM((share, 2, rows, stations), jnp.bfloat16),
            pltpu.VMEM((share, stations, 2 * rows), jnp.bfloat16),
            pltpu.VMEM((2, height + 16, stations), jnp.float32),
            pltpu.VMEM((height, stations), jnp.float32),
            pltpu.VMEM((2, height, rows), jnp.float32),
            pltpu.SemaphoreType.DMA((depth,)),
            pltpu.SemaphoreType.DMA((depth,)),
            pltpu.SemaphoreType.DMA((depth, 3, 3)),
            pltpu.SemaphoreType.DMA((depth, 3, 3)),
            pltpu.SemaphoreType.DMA((depth, 2, 3)),
            pltpu.SemaphoreType.DMA((depth, 2, 3)),
            pltpu.SemaphoreType.DMA((share,)),
            pltpu.SemaphoreType.DMA((3, stat_count)),
            pltpu.SemaphoreType.DMA((2, 3, stat_count)),
        ],
        compiler_params=pltpu.CompilerParams(
            collective_id=0, has_side_effects=True, vmem_limit_bytes=32 * 1024 * 1024
        ),
        cost_estimate=pl.CostEstimate(
            flops=2 * 3 * 2 * 512 * 1024 * 1024, bytes_accessed=12 << 20, transcendentals=0
        ),
    )(own, receive_permutation())


def local(voltages, taps):
    table = dft_rows(CHANNELS, 32, 4, 3)
    sent = channelize(voltages, taps, table).reshape(256, 3, 16, 128)
    own = lax.all_to_all(sent, ("stat", "chan"), 0, 0, tiled=True)
    vis, gains = correlate_and_solve(own)
    return vis, gains.reshape(12, 2, 128)


def solution(mesh):
    placed = (P(None, ("stat", "chan"), None, None), P())
    return jax.shard_map(
        local,
        mesh=mesh,
        in_specs=placed,
        out_specs=(P("chan", None, "stat", None), P("chan", None, "stat")),
        check_vma=False,
    )
```

```python
import functools
import math

import jax
import jax.numpy as jnp
import numpy as np
from jax import lax
from jax.experimental import pallas as pl
from jax.experimental.pallas import tpu as pltpu
from jax.sharding import PartitionSpec as P

CHANNELS = 384
STATIONS = 1024
FILTER_TAPS = 12
SPECTRA = 512
GAIN_ITERS = 8
SMOOTH_HALF = 3
EPSILON = 1e-06

MESH = pl.DeviceIdType.MESH
NT = (((1,), (1,)), ((), ()))


def dft_rows(length, groups, depth, share):
    index = np.arange(length)
    angle = (index[:, None] * index[None, :] % length) * (2.0 * math.pi / length)
    cosine = np.cos(angle) / math.sqrt(length)
    sine = np.sin(angle) / math.sqrt(length)
    real_row = np.concatenate([cosine, sine], 1)
    imag_row = np.concatenate([-sine, cosine], 1)
    rows = np.stack([real_row, imag_row], 1)
    rows = rows.reshape(groups, depth, share, 2, 2 * length).transpose(1, 0, 2, 3, 4)
    return jnp.asarray(rows.reshape(2 * length, 2 * length), jnp.bfloat16)


def send_permutation():
    matrix = np.zeros((256, 256), np.float32)
    for p in range(4):
        for th in range(2):
            for k in range(16):
                for a in range(2):
                    matrix[k * 16 + (a * 4 + p) * 2 + th, (p * 2 + th) * 32 + k * 2 + a] = 1.0
    return jnp.asarray(matrix, jnp.bfloat16)


def receive_permutation():
    matrix = np.zeros((256, 256), np.float32)
    for s in range(16):
        for a in range(2):
            for p in range(4):
                for th in range(2):
                    matrix[(a * 2 + th) * 64 + s * 4 + p, s * 16 + (a * 4 + p) * 2 + th] = 1.0
    return jnp.asarray(matrix, jnp.bfloat16)


def channelize_kernel(volt_ref, taps_ref, table_ref, perm_ref, out_ref, wide, filt, stage):
    station = pl.program_id(0)
    frames = SPECTRA + FILTER_TAPS - 1
    for part in range(2):
        for lane in range(CHANNELS // 128):
            wide[lane, pl.ds(0, frames), :] = volt_ref[part, 0, :, pl.ds(lane * 128, 128)].astype(
                jnp.float32
            )
        for lane in range(CHANNELS // 128):
            weights = [taps_ref[pl.ds(j, 1), pl.ds(lane * 128, 128)] for j in range(FILTER_TAPS)]

            def rows(step, _, part=part, lane=lane, weights=weights):
                base = step * 128
                total = weights[0] * wide[lane, pl.ds(base, 128), :]
                for j in range(1, FILTER_TAPS):
                    total = total + weights[j] * wide[lane, pl.ds(base + j, 128), :]
                filt[pl.ds(base, 128), pl.ds(part * CHANNELS + lane * 128, 128)] = total.astype(
                    jnp.bfloat16
                )
                return 0

            for step in range(SPECTRA // 128):
                rows(step, 0)
    for block in range(1):
        spectra = lax.dot_general(
            table_ref[pl.ds(block * 768, 768), :],
            filt[...],
            NT,
            preferred_element_type=jnp.float32,
        ).astype(jnp.bfloat16)
        for th in range(2):
            for core in range(2):
                stage[station * 2 + th, pl.ds(block * 768, 768), pl.ds(core * 128, 128)] = spectra[
                    :, (core * 2 + th) * 128 : (core * 2 + th) * 128 + 128
                ]

    @pl.when(station == 3)
    def _():
        for group in range(24):
            rows = jnp.concatenate(
                [stage[i, pl.ds(group * 32, 32), :] for i in range(8)], axis=0
            )
            turned = jnp.dot(
                perm_ref[...], rows, preferred_element_type=jnp.float32
            ).astype(jnp.bfloat16)
            depth, first = group // 6, (group % 6) * 16
            for core in range(2):
                out_ref[depth, core, pl.ds(first, 16)] = turned[
                    :, core * 128 : core * 128 + 128
                ].reshape(16, 16, 128)


def channelize(voltages, taps, table):
    frames = voltages.shape[2]
    return pl.pallas_call(
        channelize_kernel,
        grid=(4,),
        out_shape=jax.ShapeDtypeStruct((4, 2, 96, 16, 128), jnp.bfloat16),
        in_specs=[
            pl.BlockSpec((2, 1, frames, CHANNELS), lambda i: (0, i, 0, 0)),
            pl.BlockSpec((FILTER_TAPS, CHANNELS), lambda i: (0, 0)),
            pl.BlockSpec((2 * CHANNELS, 2 * CHANNELS), lambda i: (0, 0)),
            pl.BlockSpec((256, 256), lambda i: (0, 0)),
        ],
        out_specs=pl.BlockSpec((4, 2, 96, 16, 128), lambda i: (0, 0, 0, 0, 0)),
        scratch_shapes=[
            pltpu.VMEM((CHANNELS // 128, 528, 128), jnp.float32),
            pltpu.VMEM((SPECTRA, 2 * CHANNELS), jnp.bfloat16),
            pltpu.VMEM((8, 2 * CHANNELS, 256), jnp.bfloat16),
        ],
        compiler_params=pltpu.CompilerParams(vmem_limit_bytes=48 * 1024 * 1024),
        cost_estimate=pl.CostEstimate(
            flops=2 * 2048 * 768 * 768, bytes_accessed=8 << 20, transcendentals=0
        ),
    )(voltages, taps, table, send_permutation())


def exchange_kernel(
    stat_count,
    chan_count,
    own_ref,
    perm_ref,
    out_ref,
    gains_ref,
    other,
    held,
    stage,
    flip,
    vis,
    turned,
    padded,
    gains,
    diag,
    pair_send,
    pair_recv,
    vis_send,
    vis_recv,
    flip_send,
    flip_recv,
    out_sem,
    send_sem,
    recv_sem,
):
    sources, depth = own_ref.shape[0], own_ref.shape[1]
    share, _, rows, stations = vis.shape
    height = 2 * share
    total = chan_count * share
    stat = lax.axis_index("stat")
    chan = lax.axis_index("chan")
    line, core = stat // 2, stat % 2
    has_low, has_high = chan > 0, chan < chan_count - 1
    peers = [lax.rem(stat + j, stat_count) for j in range(stat_count)]

    def partner(d):
        return 2 * ((line // 2 + (1, 1, 0, 0)[d]) % 2) + (line % 2 + (0, 1, 1, 0)[d]) % 2

    for slot in range(2):
        padded[slot, pl.ds(0, 8), :] = jnp.zeros((8, stations), jnp.float32)
        padded[slot, pl.ds(height + 8, 8), :] = jnp.zeros((8, stations), jnp.float32)
    barrier = pltpu.get_barrier_semaphore()
    for first, present, step in ((1, None, 0), (0, has_low, -1), (0, has_high, 1)):

        def greet(first=first, step=step):
            for j in range(first, stat_count):
                pl.semaphore_signal(
                    barrier, inc=1, device_id=(peers[j], chan + step), device_id_type=MESH
                )

        greet() if present is None else pl.when(present)(greet)
    sides = has_low.astype(jnp.int32) + has_high.astype(jnp.int32)
    pl.semaphore_wait(barrier, stat_count - 1 + stat_count * sides)

    def pair_copy(c):
        return pltpu.make_async_remote_copy(
            src_ref=own_ref.at[:, c],
            dst_ref=other.at[c],
            send_sem=pair_send.at[c],
            recv_sem=pair_recv.at[c],
            device_id=(line * 2 + 1 - core, chan),
            device_id_type=MESH,
        )

    pair_copy(0).start()

    def assemble(half, source):
        def group(step, _):
            first = pl.multiple_of(step * 16, 16)
            block = source[pl.ds(first, 16)].reshape(256, 128)
            moved = jnp.dot(perm_ref[...], block, preferred_element_type=jnp.float32).astype(
                jnp.bfloat16
            )
            place = pl.ds(pl.multiple_of(step * 64, 64), 64)
            for quarter in range(4):
                held[place, pl.ds((half * 4 + quarter) * 128, 128)] = moved[
                    quarter * 64 : quarter * 64 + 64
                ]
            return 0

        lax.fori_loop(0, sources // 16, group, 0)

    inner = (line + 1) // 2 % 2 == 1
    outer = jnp.logical_not(inner)
    first_core, second_core = core == 0, core == 1

    def columns_of(place, width):
        return pl.ds(pl.multiple_of(place * rows, rows), width * rows)

    def vis_copy(c, d, kind, sending):
        target = partner(d) if sending else line
        columns = (
            columns_of(4 * (1 - target // 2), 4),
            columns_of(2 * target, 2),
            columns_of(2 * target + 1, 1),
            columns_of(2 * (target + 1 - 2 * (target % 2)), 2),
            pl.ds(0, stations),
        )[kind]
        place = (line if sending else partner(d)) * depth + c
        return pltpu.make_async_remote_copy(
            src_ref=stage.at[c * 3 + d, :, :, columns],
            dst_ref=vis.at[place, :, :, columns],
            send_sem=vis_send.at[c, d, (0, 1, 1, 2, 0)[kind]],
            recv_sem=vis_recv.at[c, d, (0, 1, 1, 2, 0)[kind]],
            device_id=(partner(d) * 2 + core, chan),
            device_id_type=MESH,
        )

    def vis_pieces(d, sending):
        if d == 2:
            return ((4, None),)
        meets_inner = inner if (d == 1) or not sending else outer
        return ((3, meets_inner), (1, first_core), (2, second_core), (0, None))

    def guarded(present, action):
        action() if present is None else pl.when(present)(action)

    def flip_copy(c, d, kind, sending):
        near = partner(2)
        k = partner(d) * depth + c
        if sending:
            columns = columns_of(stat, 1)
            device = (near * 2, near * 2 + 1, line * 2 + 1)[kind]
            slot = 2 if kind == 2 else core
            step = d if kind == 2 else 1 - d
        else:
            columns = columns_of((near * 2, near * 2 + 1, line * 2)[kind], 1)
            device, slot, step = stat, kind, d
        return pltpu.make_async_remote_copy(
            src_ref=flip.at[c, d, kind],
            dst_ref=vis.at[k, :, :, columns],
            send_sem=flip_send.at[c, d, kind],
            recv_sem=flip_recv.at[c, step, slot],
            device_id=(device, chan),
            device_id_type=MESH,
        )

    def send_flipped(c, d, kind):
        near = partner(2)
        columns = columns_of((near * 2, near * 2 + 1, line * 2 + 1)[kind], 1)
        k = partner(d) * depth + c
        flip[c, d, kind, 0] = vis[k, 0, :, columns].T
        flip[c, d, kind, 1] = -vis[k, 1, :, columns].T
        flip_copy(c, d, kind, True).start()

    def receive(c, d):
        if d == 2:
            vis_copy(c, d, 4, False).wait_recv()
            return

        def neighbour():
            vis_copy(c, d, 3, False).wait_recv()
            send_flipped(c, d, 0)
            send_flipped(c, d, 1)

        def pair():
            vis_copy(c, d, 1, False).wait_recv()
            send_flipped(c, d, 2)

        def from_neighbour():
            flip_copy(c, d, 0, False).wait_recv()
            flip_copy(c, d, 1, False).wait_recv()

        def from_pair():
            vis_copy(c, d, 2, False).wait_recv()
            flip_copy(c, d, 2, False).wait_recv()

        pl.when(inner)(neighbour)
        pl.when(first_core)(pair)
        vis_copy(c, d, 0, False).wait_recv()
        pl.when(outer)(from_neighbour)
        pl.when(second_core)(from_pair)

    def correlate(c, _):
        assemble(0, own_ref.at[:, c])
        pair_copy(c).wait_recv()
        pl.when(c + 1 < depth)(lambda: pair_copy(c + 1).start())
        assemble(1, other.at[c])
        for d in range(4):
            first = pl.multiple_of((partner(d) * 2 + core) * rows, rows)
            left = held[pl.ds(first, rows), :]
            pieces = []
            for half in range(2):
                base = half * 512
                pieces += [left[:, base + 256 : base + 512], -left[:, base : base + 256]]
            both = jnp.concatenate([left, jnp.concatenate(pieces, axis=1)], axis=0)

            def block(place, both=both, d=d):
                columns = columns_of(place, 2)
                product = lax.dot_general(
                    both, held[columns, :], NT, preferred_element_type=jnp.float32
                )
                result = (product * (1.0 / SPECTRA)).astype(jnp.bfloat16)
                for part in range(2):
                    piece = result[part * rows : part * rows + rows]
                    if d < 3:
                        stage[c * 3 + d, part, :, columns] = piece
                    else:
                        vis[line * depth + c, part, :, columns] = piece

            if d < 2:
                target = partner(d)
                for kind, present in vis_pieces(d, True):

                    def send(kind=kind, d=d, target=target, block=block):
                        if kind == 0:
                            block(4 * (1 - target // 2))
                            block(4 * (1 - target // 2) + 2)
                        elif kind == 3:
                            block(2 * (target + 1 - 2 * (target % 2)))
                        vis_copy(c, d, kind, True).start()

                    if kind == 1:
                        block(2 * target)
                    guarded(present, send)
            else:
                for place in range(0, stat_count, 2):
                    block(place)
                if d == 2:
                    vis_copy(c, d, 4, True).start()
        return 0

    lax.fori_loop(0, depth, correlate, 0)

    own = pl.ds(pl.multiple_of(stat * rows, rows), rows)
    row = lax.broadcasted_iota(jnp.int32, (height, 1), 0)
    even = row % 2 == 0
    sign = jnp.where(even, -1.0, 1.0)
    channel = chan * share + row // 2
    weight = jnp.zeros((height, 1), jnp.float32)
    for m in range(-SMOOTH_HALF, SMOOTH_HALF + 1):
        inside = jnp.logical_and(channel + m >= 0, channel + m < total)
        weight = weight + jnp.where(inside, 1.0 / (1.0 + abs(m)), 0.0)

    def swap(x):
        return jnp.where(even, pltpu.roll(x, height - 1, 0), pltpu.roll(x, 1, 0))

    eye = lax.broadcasted_iota(jnp.int32, (rows, rows), 0) == lax.broadcasted_iota(
        jnp.int32, (rows, rows), 1
    )

    def split(g):
        one = g.astype(jnp.bfloat16).astype(jnp.float32)
        rest = g - one
        two = rest.astype(jnp.bfloat16).astype(jnp.float32)
        three = rest - two
        return jnp.concatenate(
            [one, two, three, jnp.zeros((8, stations), jnp.float32)], axis=0
        ).astype(jnp.bfloat16)

    def multiply(left, k, real, imag):
        product = jnp.dot(left, turned[k], preferred_element_type=jnp.float32)
        product = (
            product[0:height] + product[height : 2 * height] + product[2 * height : 3 * height]
        )
        mine = row // 2 == k
        return jnp.where(mine, product[:, :rows], real), jnp.where(mine, product[:, rows:], imag)

    def out_copy(k):
        return pltpu.make_async_copy(vis.at[k], out_ref.at[k], out_sem.at[k])

    gains[...] = jnp.broadcast_to(jnp.where(even, 1.0, 0.0), (height, stations))
    left = split(gains[...])
    zero = jnp.zeros((height, rows), jnp.float32)

    def arrive(c, carry):
        real, imag, diag_real, diag_imag = carry
        for d in (3, 2, 0, 1):
            if d < 3:
                receive(c, d)
            k = partner(d) * depth + c
            out_copy(k).start()
            turned[k] = vis[k].reshape(2 * rows, stations).T
            mine = row // 2 == k
            lines = [
                jnp.sum(
                    jnp.where(eye, vis[k, part, :, own].astype(jnp.float32), 0.0),
                    axis=0,
                    keepdims=True,
                )
                for part in range(2)
            ]
            diag_real = jnp.where(mine, lines[0], diag_real)
            diag_imag = jnp.where(mine, lines[1], diag_imag)
            real, imag = multiply(left, k, real, imag)
        return real, imag, diag_real, diag_imag

    real, imag, diag_real, diag_imag = lax.fori_loop(0, depth, arrive, (zero, zero, zero, zero))
    diag[0] = diag_real
    diag[1] = sign * diag_imag

    def finish(odd, real, imag, every):
        mine = gains[:, own]
        y = real + sign * swap(imag) - (diag[0] * mine + diag[1] * swap(mine))
        power = mine * mine
        power = power + swap(power)
        u = y / (every - power + EPSILON)
        return 0.5 * (u + mine) if odd else u

    def power_of(g):
        every = jnp.broadcast_to(jnp.sum(g * g, axis=1, keepdims=True), (height, rows))
        return every + swap(every)

    def copies(slot, kind, j):
        middle = (slot, pl.ds(8, height), own)
        source = [middle, (slot, pl.ds(8, 8), own), (slot, pl.ds(height, 8), own)][kind]
        target = [middle, (slot, pl.ds(height + 8, 8), own), (slot, pl.ds(0, 8), own)][kind]
        return pltpu.make_async_remote_copy(
            src_ref=padded.at[source],
            dst_ref=padded.at[target],
            send_sem=send_sem.at[kind],
            recv_sem=recv_sem.at[slot, kind],
            device_id=(peers[j], chan + (0, -1, 1)[kind]),
            device_id_type=MESH,
        )

    def all_copies(slot, kind, count):
        where = (
            slot,
            (pl.ds(8, height), pl.ds(height + 8, 8), pl.ds(0, 8))[kind],
            pl.ds(0, count * rows),
        )
        return pltpu.make_async_remote_copy(
            src_ref=padded.at[where],
            dst_ref=padded.at[where],
            send_sem=send_sem.at[kind],
            recv_sem=recv_sem.at[slot, kind],
            device_id=(peers[1], chan),
            device_id_type=MESH,
        )

    def start(slot, kinds):
        for kind, steps, present in kinds:

            def send(kind=kind, steps=steps):
                for j in steps:
                    copies(slot, kind, j).start()

            guarded(present, send)

    def finish_copies(slot, kinds):
        for kind, steps, present in kinds:
            arriving = (0, 2, 1)[kind]
            guarded(present, lambda: all_copies(slot, arriving, len(steps)).wait_recv())
        for kind, steps, present in kinds:
            guarded(present, lambda: all_copies(slot, kind, len(steps)).wait_send())

    def smooth(slot, columns):
        summed = None
        for m in range(-SMOOTH_HALF, SMOOTH_HALF + 1):
            term = (1.0 / (1.0 + abs(m))) * padded[slot, pl.ds(8 + 2 * m, height), columns]
            summed = term if summed is None else summed + term
        return summed / weight

    everyone = list(range(stat_count))
    halo = ((1, everyone, has_low), (2, everyone, has_high))
    group = ((0, everyone[1:], None),)
    edge = ((1, [0], has_low), (2, [0], has_high))
    outer_channels = [k for k in range(share) if k < 4 or k >= share - 4]
    inner_channels = [k for k in range(share) if k not in outer_channels]

    def settle(slot):
        finish_copies(slot, halo + group)
        g = smooth(slot, pl.ds(0, stations))
        gains[...] = g
        return g

    def iterate(slot, g, last=False):
        left = split(g)
        every = power_of(g)
        real, imag = zero, zero
        for k in outer_channels:
            real, imag = multiply(left, k, real, imag)
        u = finish(slot == 1, real, imag, every)
        padded[slot, pl.ds(8, 8), own] = u[0:8]
        padded[slot, pl.ds(height, 8), own] = u[height - 8 : height]
        start(slot, edge if last else halo)
        for k in inner_channels:
            real, imag = multiply(left, k, real, imag)
        u = finish(slot == 1, real, imag, every)
        padded[slot, pl.ds(16, height - 16), own] = u[8 : height - 8]
        if last:
            finish_copies(slot, edge)
            return None
        start(slot, group)
        return settle(slot)

    padded[0, pl.ds(8, height), own] = finish(False, real, imag, power_of(gains[...]))
    start(0, halo + group)
    g = settle(0)
    g = lax.fori_loop(0, (GAIN_ITERS - 2) // 2, lambda _, g: iterate(0, iterate(1, g)), g)
    iterate(1, g, True)
    gains_ref[...] = smooth(1, own)
    for c in range(depth):
        pair_copy(c).wait_send()
        for d in range(3):
            for kind, present in vis_pieces(d, True):
                guarded(present, lambda: vis_copy(c, d, kind, True).wait_send())
        for d in range(2):
            for kind, present in ((0, inner), (1, inner), (2, first_core)):
                guarded(present, lambda: flip_copy(c, d, kind, True).wait_send())
    for k in range(share):
        out_copy(k).wait()


def correlate_and_solve(own):
    sources, depth = own.shape[:2]
    stations = 4 * sources
    stat_count, chan_count = lax.axis_size("stat"), lax.axis_size("chan")
    share, rows = 4 * depth, stations // stat_count
    height = 2 * share
    return pl.pallas_call(
        functools.partial(exchange_kernel, stat_count, chan_count),
        out_shape=(
            jax.ShapeDtypeStruct((share, 2, rows, stations), jnp.bfloat16),
            jax.ShapeDtypeStruct((height, rows), jnp.float32),
        ),
        in_specs=[pl.BlockSpec(memory_space=pltpu.VMEM)] * 2,
        out_specs=(
            pl.BlockSpec(memory_space=pl.ANY),
            pl.BlockSpec(memory_space=pltpu.VMEM),
        ),
        scratch_shapes=[
            pltpu.VMEM((depth, sources, 16, 128), jnp.bfloat16),
            pltpu.VMEM((stations, 2 * SPECTRA), jnp.bfloat16),
            pltpu.VMEM((3 * depth, 2, rows, stations), jnp.bfloat16),
            pltpu.VMEM((depth, 2, 3, 2, rows, rows), jnp.bfloat16),
            pltpu.VMEM((share, 2, rows, stations), jnp.bfloat16),
            pltpu.VMEM((share, stations, 2 * rows), jnp.bfloat16),
            pltpu.VMEM((2, height + 16, stations), jnp.float32),
            pltpu.VMEM((height, stations), jnp.float32),
            pltpu.VMEM((2, height, rows), jnp.float32),
            pltpu.SemaphoreType.DMA((depth,)),
            pltpu.SemaphoreType.DMA((depth,)),
            pltpu.SemaphoreType.DMA((depth, 3, 3)),
            pltpu.SemaphoreType.DMA((depth, 3, 3)),
            pltpu.SemaphoreType.DMA((depth, 2, 3)),
            pltpu.SemaphoreType.DMA((depth, 2, 3)),
            pltpu.SemaphoreType.DMA((share,)),
            pltpu.SemaphoreType.DMA((3,)),
            pltpu.SemaphoreType.DMA((2, 3)),
        ],
        compiler_params=pltpu.CompilerParams(
            collective_id=0, has_side_effects=True, vmem_limit_bytes=32 * 1024 * 1024
        ),
        cost_estimate=pl.CostEstimate(
            flops=2 * 3 * 2 * 512 * 1024 * 1024, bytes_accessed=12 << 20, transcendentals=0
        ),
    )(own, receive_permutation())


def local(voltages, taps):
    table = dft_rows(CHANNELS, 32, 4, 3)
    sent = channelize(voltages, taps, table).reshape(256, 3, 16, 128)
    own = lax.all_to_all(sent, ("stat", "chan"), 0, 0, tiled=True)
    vis, gains = correlate_and_solve(own)
    return vis, gains.reshape(12, 2, 128)


def solution(mesh):
    placed = (P(None, ("stat", "chan"), None, None), P())
    return jax.shard_map(
        local,
        mesh=mesh,
        in_specs=placed,
        out_specs=(P("chan", None, "stat", None), P("chan", None, "stat")),
        check_vma=False,
    )
```

```python
import functools
import math

import jax
import jax.numpy as jnp
import numpy as np
from jax import lax
from jax.experimental import pallas as pl
from jax.experimental.pallas import tpu as pltpu
from jax.sharding import PartitionSpec as P

CHANNELS = 384
STATIONS = 1024
FILTER_TAPS = 12
SPECTRA = 512
GAIN_ITERS = 8
SMOOTH_HALF = 3
EPSILON = 1e-06

MESH = pl.DeviceIdType.MESH
NT = (((1,), (1,)), ((), ()))


def dft_rows(length, groups, depth, share):
    index = np.arange(length)
    angle = (index[:, None] * index[None, :] % length) * (2.0 * math.pi / length)
    cosine = np.cos(angle) / math.sqrt(length)
    sine = np.sin(angle) / math.sqrt(length)
    real_row = np.concatenate([cosine, sine], 1)
    imag_row = np.concatenate([-sine, cosine], 1)
    rows = np.stack([real_row, imag_row], 1)
    rows = rows.reshape(groups, depth, share, 2, 2 * length).transpose(1, 0, 2, 3, 4)
    return jnp.asarray(rows.reshape(2 * length, 2 * length), jnp.bfloat16)


def send_permutation():
    matrix = np.zeros((256, 256), np.float32)
    for p in range(4):
        for th in range(2):
            for k in range(16):
                for a in range(2):
                    matrix[k * 16 + (a * 4 + p) * 2 + th, (p * 2 + th) * 32 + k * 2 + a] = 1.0
    return jnp.asarray(matrix, jnp.bfloat16)


def receive_permutation():
    matrix = np.zeros((256, 256), np.float32)
    for s in range(16):
        for a in range(2):
            for p in range(4):
                for th in range(2):
                    matrix[(a * 2 + th) * 64 + s * 4 + p, s * 16 + (a * 4 + p) * 2 + th] = 1.0
    return jnp.asarray(matrix, jnp.bfloat16)


def channelize_kernel(volt_ref, taps_ref, table_ref, perm_ref, out_ref, wide, filt, stage):
    station = pl.program_id(0)
    frames = SPECTRA + FILTER_TAPS - 1
    for part in range(2):
        for lane in range(CHANNELS // 128):
            wide[lane, pl.ds(0, frames), :] = volt_ref[part, 0, :, pl.ds(lane * 128, 128)].astype(
                jnp.float32
            )
        for lane in range(CHANNELS // 128):
            weights = [taps_ref[pl.ds(j, 1), pl.ds(lane * 128, 128)] for j in range(FILTER_TAPS)]

            def rows(step, _, part=part, lane=lane, weights=weights):
                base = step * 128
                total = weights[0] * wide[lane, pl.ds(base, 128), :]
                for j in range(1, FILTER_TAPS):
                    total = total + weights[j] * wide[lane, pl.ds(base + j, 128), :]
                filt[pl.ds(base, 128), pl.ds(part * CHANNELS + lane * 128, 128)] = total.astype(
                    jnp.bfloat16
                )
                return 0

            for step in range(SPECTRA // 128):
                rows(step, 0)
    for block in range(1):
        spectra = lax.dot_general(
            table_ref[pl.ds(block * 768, 768), :],
            filt[...],
            NT,
            preferred_element_type=jnp.float32,
        ).astype(jnp.bfloat16)
        for th in range(2):
            for core in range(2):
                stage[station * 2 + th, pl.ds(block * 768, 768), pl.ds(core * 128, 128)] = spectra[
                    :, (core * 2 + th) * 128 : (core * 2 + th) * 128 + 128
                ]

    @pl.when(station == 3)
    def _():
        for group in range(24):
            rows = jnp.concatenate(
                [stage[i, pl.ds(group * 32, 32), :] for i in range(8)], axis=0
            )
            turned = jnp.dot(
                perm_ref[...], rows, preferred_element_type=jnp.float32
            ).astype(jnp.bfloat16)
            depth, first = group // 6, (group % 6) * 16
            for core in range(2):
                out_ref[depth, core, pl.ds(first, 16)] = turned[
                    :, core * 128 : core * 128 + 128
                ].reshape(16, 16, 128)


def channelize(voltages, taps, table):
    frames = voltages.shape[2]
    return pl.pallas_call(
        channelize_kernel,
        grid=(4,),
        out_shape=jax.ShapeDtypeStruct((4, 2, 96, 16, 128), jnp.bfloat16),
        in_specs=[
            pl.BlockSpec((2, 1, frames, CHANNELS), lambda i: (0, i, 0, 0)),
            pl.BlockSpec(memory_space=pltpu.VMEM),
            pl.BlockSpec(memory_space=pltpu.VMEM),
            pl.BlockSpec(memory_space=pltpu.VMEM),
        ],
        out_specs=pl.BlockSpec(memory_space=pltpu.VMEM),
        scratch_shapes=[
            pltpu.VMEM((CHANNELS // 128, 528, 128), jnp.float32),
            pltpu.VMEM((SPECTRA, 2 * CHANNELS), jnp.bfloat16),
            pltpu.VMEM((8, 2 * CHANNELS, 256), jnp.bfloat16),
        ],
        compiler_params=pltpu.CompilerParams(vmem_limit_bytes=48 * 1024 * 1024),
        cost_estimate=pl.CostEstimate(
            flops=2 * 2048 * 768 * 768, bytes_accessed=8 << 20, transcendentals=0
        ),
    )(voltages, taps, table, send_permutation())


def exchange_kernel(
    stat_count,
    chan_count,
    own_ref,
    perm_ref,
    out_ref,
    gains_ref,
    other,
    held,
    stage,
    flip,
    vis,
    turned,
    padded,
    gains,
    diag,
    pair_send,
    pair_recv,
    vis_send,
    vis_recv,
    flip_send,
    flip_recv,
    out_sem,
    send_sem,
    recv_sem,
):
    sources, depth = own_ref.shape[0], own_ref.shape[1]
    share, _, rows, stations = vis.shape
    height = 2 * share
    total = chan_count * share
    stat = lax.axis_index("stat")
    chan = lax.axis_index("chan")
    line, core = stat // 2, stat % 2
    has_low, has_high = chan > 0, chan < chan_count - 1
    peers = [lax.rem(stat + j, stat_count) for j in range(stat_count)]

    def partner(d):
        return 2 * ((line // 2 + (1, 1, 0, 0)[d]) % 2) + (line % 2 + (0, 1, 1, 0)[d]) % 2

    for slot in range(2):
        for place in range(stat_count):
            padded[slot, place, pl.ds(0, 8), :] = jnp.zeros((8, rows), jnp.float32)
            padded[slot, place, pl.ds(height + 8, 8), :] = jnp.zeros((8, rows), jnp.float32)
    barrier = pltpu.get_barrier_semaphore()
    for first, present, step in ((1, None, 0), (0, has_low, -1), (0, has_high, 1)):

        def greet(first=first, step=step):
            for j in range(first, stat_count):
                pl.semaphore_signal(
                    barrier, inc=1, device_id=(peers[j], chan + step), device_id_type=MESH
                )

        greet() if present is None else pl.when(present)(greet)
    sides = has_low.astype(jnp.int32) + has_high.astype(jnp.int32)
    pl.semaphore_wait(barrier, stat_count - 1 + stat_count * sides)

    def pair_copy(c):
        return pltpu.make_async_remote_copy(
            src_ref=own_ref.at[:, c],
            dst_ref=other.at[c],
            send_sem=pair_send.at[c],
            recv_sem=pair_recv.at[c],
            device_id=(line * 2 + 1 - core, chan),
            device_id_type=MESH,
        )

    pair_copy(0).start()

    def assemble(half, source):
        def group(step, _):
            first = pl.multiple_of(step * 16, 16)
            block = source[pl.ds(first, 16)].reshape(256, 128)
            moved = jnp.dot(perm_ref[...], block, preferred_element_type=jnp.float32).astype(
                jnp.bfloat16
            )
            place = pl.ds(pl.multiple_of(step * 64, 64), 64)
            for quarter in range(4):
                held[place, pl.ds((half * 4 + quarter) * 128, 128)] = moved[
                    quarter * 64 : quarter * 64 + 64
                ]
            return 0

        lax.fori_loop(0, sources // 16, group, 0)

    inner = (line + 1) // 2 % 2 == 1
    outer = jnp.logical_not(inner)
    first_core, second_core = core == 0, core == 1

    def columns_of(place, width):
        return pl.ds(pl.multiple_of(place * rows, rows), width * rows)

    def vis_copy(c, d, kind, sending):
        target = partner(d) if sending else line
        columns = (
            columns_of(4 * (1 - target // 2), 4),
            columns_of(2 * target, 2),
            columns_of(2 * target + 1, 1),
            columns_of(2 * (target + 1 - 2 * (target % 2)), 2),
            pl.ds(0, stations),
        )[kind]
        place = (line if sending else partner(d)) * depth + c
        return pltpu.make_async_remote_copy(
            src_ref=stage.at[c * 3 + d, :, :, columns],
            dst_ref=vis.at[place, :, :, columns],
            send_sem=vis_send.at[c, d, (0, 1, 1, 2, 0)[kind]],
            recv_sem=vis_recv.at[c, d, (0, 1, 1, 2, 0)[kind]],
            device_id=(partner(d) * 2 + core, chan),
            device_id_type=MESH,
        )

    def vis_pieces(d, sending):
        if d == 2:
            return ((4, None),)
        meets_inner = inner if (d == 1) or not sending else outer
        return ((3, meets_inner), (1, first_core), (2, second_core), (0, None))

    def guarded(present, action):
        action() if present is None else pl.when(present)(action)

    def flip_copy(c, d, kind, sending):
        near = partner(2)
        k = partner(d) * depth + c
        if sending:
            columns = columns_of(stat, 1)
            device = (near * 2, near * 2 + 1, line * 2 + 1)[kind]
            slot = 2 if kind == 2 else core
            step = d if kind == 2 else 1 - d
        else:
            columns = columns_of((near * 2, near * 2 + 1, line * 2)[kind], 1)
            device, slot, step = stat, kind, d
        return pltpu.make_async_remote_copy(
            src_ref=flip.at[c, d, kind],
            dst_ref=vis.at[k, :, :, columns],
            send_sem=flip_send.at[c, d, kind],
            recv_sem=flip_recv.at[c, step, slot],
            device_id=(device, chan),
            device_id_type=MESH,
        )

    def send_flipped(c, d, kind):
        near = partner(2)
        columns = columns_of((near * 2, near * 2 + 1, line * 2 + 1)[kind], 1)
        k = partner(d) * depth + c
        flip[c, d, kind, 0] = vis[k, 0, :, columns].T
        flip[c, d, kind, 1] = -vis[k, 1, :, columns].T
        flip_copy(c, d, kind, True).start()

    def receive(c, d):
        if d == 2:
            vis_copy(c, d, 4, False).wait_recv()
            return

        def neighbour():
            vis_copy(c, d, 3, False).wait_recv()
            send_flipped(c, d, 0)
            send_flipped(c, d, 1)

        def pair():
            vis_copy(c, d, 1, False).wait_recv()
            send_flipped(c, d, 2)

        def from_neighbour():
            flip_copy(c, d, 0, False).wait_recv()
            flip_copy(c, d, 1, False).wait_recv()

        def from_pair():
            vis_copy(c, d, 2, False).wait_recv()
            flip_copy(c, d, 2, False).wait_recv()

        pl.when(inner)(neighbour)
        pl.when(first_core)(pair)
        vis_copy(c, d, 0, False).wait_recv()
        pl.when(outer)(from_neighbour)
        pl.when(second_core)(from_pair)

    def correlate(c, _):
        assemble(0, own_ref.at[:, c])
        pair_copy(c).wait_recv()
        pl.when(c + 1 < depth)(lambda: pair_copy(c + 1).start())
        assemble(1, other.at[c])
        for d in range(4):
            first = pl.multiple_of((partner(d) * 2 + core) * rows, rows)
            left = held[pl.ds(first, rows), :]
            pieces = []
            for half in range(2):
                base = half * 512
                pieces += [left[:, base + 256 : base + 512], -left[:, base : base + 256]]
            both = jnp.concatenate([left, jnp.concatenate(pieces, axis=1)], axis=0)

            def block(place, both=both, d=d):
                columns = columns_of(place, 2)
                product = lax.dot_general(
                    both, held[columns, :], NT, preferred_element_type=jnp.float32
                )
                result = (product * (1.0 / SPECTRA)).astype(jnp.bfloat16)
                for part in range(2):
                    piece = result[part * rows : part * rows + rows]
                    if d < 3:
                        stage[c * 3 + d, part, :, columns] = piece
                    else:
                        vis[line * depth + c, part, :, columns] = piece

            if d < 2:
                target = partner(d)
                for kind, present in vis_pieces(d, True):

                    def send(kind=kind, d=d, target=target, block=block):
                        if kind == 0:
                            block(4 * (1 - target // 2))
                            block(4 * (1 - target // 2) + 2)
                        elif kind == 3:
                            block(2 * (target + 1 - 2 * (target % 2)))
                        vis_copy(c, d, kind, True).start()

                    if kind == 1:
                        block(2 * target)
                    guarded(present, send)
            else:
                for place in range(0, stat_count, 2):
                    block(place)
                if d == 2:
                    vis_copy(c, d, 4, True).start()
        return 0

    lax.fori_loop(0, depth, correlate, 0)

    own = pl.ds(pl.multiple_of(stat * rows, rows), rows)
    row = lax.broadcasted_iota(jnp.int32, (height, 1), 0)
    even = row % 2 == 0
    sign = jnp.where(even, -1.0, 1.0)
    channel = chan * share + row // 2
    weight = jnp.zeros((height, 1), jnp.float32)
    for m in range(-SMOOTH_HALF, SMOOTH_HALF + 1):
        inside = jnp.logical_and(channel + m >= 0, channel + m < total)
        weight = weight + jnp.where(inside, 1.0 / (1.0 + abs(m)), 0.0)

    def swap(x):
        return jnp.where(even, pltpu.roll(x, height - 1, 0), pltpu.roll(x, 1, 0))

    eye = lax.broadcasted_iota(jnp.int32, (rows, rows), 0) == lax.broadcasted_iota(
        jnp.int32, (rows, rows), 1
    )

    def split(g):
        one = g.astype(jnp.bfloat16).astype(jnp.float32)
        rest = g - one
        two = rest.astype(jnp.bfloat16).astype(jnp.float32)
        three = rest - two
        return jnp.concatenate(
            [one, two, three, jnp.zeros((8, stations), jnp.float32)], axis=0
        ).astype(jnp.bfloat16)

    def multiply(left, k, real, imag):
        product = jnp.dot(left, turned[k], preferred_element_type=jnp.float32)
        product = (
            product[0:height] + product[height : 2 * height] + product[2 * height : 3 * height]
        )
        mine = row // 2 == k
        return jnp.where(mine, product[:, :rows], real), jnp.where(mine, product[:, rows:], imag)

    def out_copy(k):
        return pltpu.make_async_copy(vis.at[k], out_ref.at[k], out_sem.at[k])

    gains[...] = jnp.broadcast_to(jnp.where(even, 1.0, 0.0), (height, stations))
    left = split(gains[...])
    zero = jnp.zeros((height, rows), jnp.float32)

    def arrive(c, carry):
        real, imag, diag_real, diag_imag = carry
        for d in (3, 2, 0, 1):
            if d < 3:
                receive(c, d)
            k = partner(d) * depth + c
            out_copy(k).start()
            turned[k] = vis[k].reshape(2 * rows, stations).T
            mine = row // 2 == k
            lines = [
                jnp.sum(
                    jnp.where(eye, vis[k, part, :, own].astype(jnp.float32), 0.0),
                    axis=0,
                    keepdims=True,
                )
                for part in range(2)
            ]
            diag_real = jnp.where(mine, lines[0], diag_real)
            diag_imag = jnp.where(mine, lines[1], diag_imag)
            real, imag = multiply(left, k, real, imag)
        return real, imag, diag_real, diag_imag

    real, imag, diag_real, diag_imag = lax.fori_loop(0, depth, arrive, (zero, zero, zero, zero))
    diag[0] = diag_real
    diag[1] = sign * diag_imag

    def finish(odd, real, imag, every):
        mine = gains[:, own]
        y = real + sign * swap(imag) - (diag[0] * mine + diag[1] * swap(mine))
        power = mine * mine
        power = power + swap(power)
        u = y / (every - power + EPSILON)
        return 0.5 * (u + mine) if odd else u

    def power_of(g):
        every = jnp.broadcast_to(jnp.sum(g * g, axis=1, keepdims=True), (height, rows))
        return every + swap(every)

    def copies(slot, kind, j):
        middle = (slot, stat, pl.ds(8, height))
        source = [middle, (slot, stat, pl.ds(8, 8)), (slot, stat, pl.ds(height, 8))][kind]
        target = [middle, (slot, stat, pl.ds(height + 8, 8)), (slot, stat, pl.ds(0, 8))][kind]
        return pltpu.make_async_remote_copy(
            src_ref=padded.at[source],
            dst_ref=padded.at[target],
            send_sem=send_sem.at[kind],
            recv_sem=recv_sem.at[slot, kind],
            device_id=(peers[j], chan + (0, -1, 1)[kind]),
            device_id_type=MESH,
        )

    def all_copies(slot, kind, count):
        where = (
            slot,
            pl.ds(0, count),
            (pl.ds(8, height), pl.ds(height + 8, 8), pl.ds(0, 8))[kind],
        )
        return pltpu.make_async_remote_copy(
            src_ref=padded.at[where],
            dst_ref=padded.at[where],
            send_sem=send_sem.at[kind],
            recv_sem=recv_sem.at[slot, kind],
            device_id=(peers[1], chan),
            device_id_type=MESH,
        )

    def start(slot, kinds):
        for kind, steps, present in kinds:

            def send(kind=kind, steps=steps):
                for j in steps:
                    copies(slot, kind, j).start()

            guarded(present, send)

    def finish_copies(slot, kinds):
        for kind, steps, present in kinds:
            arriving = (0, 2, 1)[kind]
            guarded(present, lambda: all_copies(slot, arriving, len(steps)).wait_recv())
        for kind, steps, present in kinds:
            guarded(present, lambda: all_copies(slot, kind, len(steps)).wait_send())

    def smooth(slot, place):
        summed = None
        for m in range(-SMOOTH_HALF, SMOOTH_HALF + 1):
            term = (1.0 / (1.0 + abs(m))) * padded[slot, place, pl.ds(8 + 2 * m, height), :]
            summed = term if summed is None else summed + term
        return summed / weight

    everyone = list(range(stat_count))
    halo = ((1, everyone, has_low), (2, everyone, has_high))
    group = ((0, everyone[1:], None),)
    edge = ((1, [0], has_low), (2, [0], has_high))
    outer_channels = [k for k in range(share) if k < 4 or k >= share - 4]
    inner_channels = [k for k in range(share) if k not in outer_channels]

    def settle(slot):
        finish_copies(slot, halo + group)
        g = jnp.concatenate([smooth(slot, place) for place in range(stat_count)], axis=1)
        gains[...] = g
        return g

    def iterate(slot, g, last=False):
        left = split(g)
        every = power_of(g)
        real, imag = zero, zero
        for k in outer_channels:
            real, imag = multiply(left, k, real, imag)
        u = finish(slot == 1, real, imag, every)
        padded[slot, stat, pl.ds(8, 8), :] = u[0:8]
        padded[slot, stat, pl.ds(height, 8), :] = u[height - 8 : height]
        start(slot, edge if last else halo)
        for k in inner_channels:
            real, imag = multiply(left, k, real, imag)
        u = finish(slot == 1, real, imag, every)
        padded[slot, stat, pl.ds(16, height - 16), :] = u[8 : height - 8]
        if last:
            finish_copies(slot, edge)
            return None
        start(slot, group)
        return settle(slot)

    padded[0, stat, pl.ds(8, height), :] = finish(False, real, imag, power_of(gains[...]))
    start(0, halo + group)
    g = settle(0)
    g = lax.fori_loop(0, (GAIN_ITERS - 2) // 2, lambda _, g: iterate(0, iterate(1, g)), g)
    iterate(1, g, True)
    gains_ref[...] = smooth(1, stat)
    for c in range(depth):
        pair_copy(c).wait_send()
        for d in range(3):
            for kind, present in vis_pieces(d, True):
                guarded(present, lambda: vis_copy(c, d, kind, True).wait_send())
        for d in range(2):
            for kind, present in ((0, inner), (1, inner), (2, first_core)):
                guarded(present, lambda: flip_copy(c, d, kind, True).wait_send())
    for k in range(share):
        out_copy(k).wait()


def correlate_and_solve(own):
    sources, depth = own.shape[:2]
    stations = 4 * sources
    stat_count, chan_count = lax.axis_size("stat"), lax.axis_size("chan")
    share, rows = 4 * depth, stations // stat_count
    height = 2 * share
    return pl.pallas_call(
        functools.partial(exchange_kernel, stat_count, chan_count),
        out_shape=(
            jax.ShapeDtypeStruct((share, 2, rows, stations), jnp.bfloat16),
            jax.ShapeDtypeStruct((height, rows), jnp.float32),
        ),
        in_specs=[pl.BlockSpec(memory_space=pltpu.VMEM)] * 2,
        out_specs=(
            pl.BlockSpec(memory_space=pl.ANY),
            pl.BlockSpec(memory_space=pltpu.VMEM),
        ),
        scratch_shapes=[
            pltpu.VMEM((depth, sources, 16, 128), jnp.bfloat16),
            pltpu.VMEM((stations, 2 * SPECTRA), jnp.bfloat16),
            pltpu.VMEM((3 * depth, 2, rows, stations), jnp.bfloat16),
            pltpu.VMEM((depth, 2, 3, 2, rows, rows), jnp.bfloat16),
            pltpu.VMEM((share, 2, rows, stations), jnp.bfloat16),
            pltpu.VMEM((share, stations, 2 * rows), jnp.bfloat16),
            pltpu.VMEM((2, stat_count, height + 16, rows), jnp.float32),
            pltpu.VMEM((height, stations), jnp.float32),
            pltpu.VMEM((2, height, rows), jnp.float32),
            pltpu.SemaphoreType.DMA((depth,)),
            pltpu.SemaphoreType.DMA((depth,)),
            pltpu.SemaphoreType.DMA((depth, 3, 3)),
            pltpu.SemaphoreType.DMA((depth, 3, 3)),
            pltpu.SemaphoreType.DMA((depth, 2, 3)),
            pltpu.SemaphoreType.DMA((depth, 2, 3)),
            pltpu.SemaphoreType.DMA((share,)),
            pltpu.SemaphoreType.DMA((3,)),
            pltpu.SemaphoreType.DMA((2, 3)),
        ],
        compiler_params=pltpu.CompilerParams(
            collective_id=0, has_side_effects=True, vmem_limit_bytes=32 * 1024 * 1024
        ),
        cost_estimate=pl.CostEstimate(
            flops=2 * 3 * 2 * 512 * 1024 * 1024, bytes_accessed=12 << 20, transcendentals=0
        ),
    )(own, receive_permutation())


def local(voltages, taps):
    table = dft_rows(CHANNELS, 32, 4, 3)
    sent = channelize(voltages, taps, table).reshape(256, 3, 16, 128)
    own = lax.all_to_all(sent, ("stat", "chan"), 0, 0, tiled=True)
    vis, gains = correlate_and_solve(own)
    return vis, gains.reshape(12, 2, 128)


def solution(mesh):
    placed = (P(None, ("stat", "chan"), None, None), P())
    return jax.shard_map(
        local,
        mesh=mesh,
        in_specs=placed,
        out_specs=(P("chan", None, "stat", None), P("chan", None, "stat")),
        check_vma=False,
    )
```
